256 devices in a mesh: dp: 8 (over z), ulysses: 32 (over y, x, core).
Axes of the slice: x: 4, y: 4, z: 8, core: 2. Of those that a mesh axis runs over, the one named last changes fastest.
Arguments:
- q_raw: bfloat16 [8, 4096, 3072], P('dp', 'ulysses')
- k_raw: bfloat16 [8, 4096, 3072], P('dp', 'ulysses')
- values: bfloat16 [8, 4096, 3072], P('dp', 'ulysses'), may hold values from -6 to 6
- grad_out: bfloat16 [8, 4096, 3072], P('dp', 'ulysses'), may hold values from -6 to 6
- q_gain: float32 [128], replicated
- k_gain: float32 [128], replicated
- block_masks: int32 [24, 32, 32], replicated, may hold values from 0 to 1, as said below
Outputs:
- grad_q_raw: bfloat16 [8, 4096, 3072], P('dp', 'ulysses')
- grad_k_raw: bfloat16 [8, 4096, 3072], P('dp', 'ulysses')
- grad_values: bfloat16 [8, 4096, 3072], P('dp', 'ulysses')
- gain_grads: float32 [2, 128], replicated
The draws below stay inside these ranges and needn't reach their ends.
Inputs may be any that keep to these rules, and one draw needn't show every extreme that they name: `block_masks`: every diagonal block is 1. A third of the heads are dense with some blocks missing, a third keep a band of neighbouring blocks, a third keep blocks a fixed stride apart; which heads are which is drawn.
All inputs are finite; a program needn't handle non-finite values.
Results may differ from the reference program's by a relative error of at most 0.0045.
The reference program's roundings to bfloat16 on the way count: a program that leaves them out, or rounds other values in their place, can miss the bound.
Values may be sent and summed in bfloat16 or wider, within the bound.
No kernel may reach another device: no remote copies, remote signals or barrier semaphores. Data moves between devices by JAX's collectives and lax.ppermute only.
A program may use at most 64 MiB of HBM per device.

```python
import jax
import jax.numpy as jnp
from jax import lax

HEADS = 24
HEAD_DIM = 128
BLOCK = 128
SEQ = 4096
VIDEOS = 8
NB = 32


def keys_float(key):
    return jax.random.normal(jax.random.fold_in(key, 31), (VIDEOS, SEQ, HEADS * HEAD_DIM), jnp.float32)


def draw_k_raw(key, part):
    return keys_float(key).astype(jnp.bfloat16)


def draw_q_raw(key, part):
    fresh = jax.random.normal(jax.random.fold_in(key, 32), (VIDEOS, SEQ, HEADS * HEAD_DIM), jnp.float32)
    return fresh.astype(jnp.bfloat16)


def draw_q_gain(key, part):
    return jax.random.uniform(jax.random.fold_in(key, 33), (HEAD_DIM,), jnp.float32, 0.5, 1.6)


def draw_k_gain(key, part):
    return jax.random.uniform(jax.random.fold_in(key, 34), (HEAD_DIM,), jnp.float32, 0.5, 1.6)


def draw_block_masks(key, part):
    base = jax.random.fold_in(key, 41)
    kinds = jax.random.permutation(jax.random.fold_in(base, 1), HEADS) % 3
    rows = jnp.arange(NB)[:, None]
    cols = jnp.arange(NB)[None, :]
    band = max(1, NB // 16)
    period = max(2, NB // 4)
    near = jnp.abs(rows - cols) <= band
    frames = (rows - cols) % period == 0
    roll = jax.random.randint(jax.random.fold_in(base, 2), (HEADS, NB, NB), 0, 10)
    kind_cube = kinds[:, None, None]
    chosen = jnp.where(kind_cube == 0, roll >= 2, jnp.where(kind_cube == 1, near[None] & (roll >= 1), frames[None] & (roll >= 1)))
    return (chosen | (rows == cols)[None]).astype(jnp.int32)


def steps_of(key, dims, shards, least, top_value):
    loudness, own = 1.0, jax.random.fold_in(key, 6)
    for axis_at, blocks in shards:
        heights = jnp.exp(jax.random.uniform(jax.random.fold_in(own, axis_at), (blocks,), jnp.float32, least / len(shards), top_value / len(shards)))
        loudness = loudness * jnp.repeat(heights, dims[axis_at] // blocks).reshape([-1 if axis == axis_at else 1 for axis in range(len(dims))])
    return loudness


def normal_values(stream_key, shape, width, reach, shards=(), dtype=jnp.bfloat16):
    values = jax.random.normal(stream_key, shape, jnp.float32) * width
    if len(shards) > 0:
        values = steps_of(stream_key, shape, shards, -0.22, 0.18) * values
    return jnp.clip(values, min=-reach, max=reach).astype(dtype)


def setup_inputs(seed: int = 0) -> dict:
    key_of = jax.random.split(jax.random.key(seed), 8)
    return {
        "q_raw": draw_q_raw(jax.random.fold_in(key_of[7], 71), 0),
        "k_raw": draw_k_raw(jax.random.fold_in(key_of[7], 71), 0),
        "values": normal_values(key_of[2], (VIDEOS, SEQ, HEADS * HEAD_DIM), 1.0, 6.0, ((0, 8), (1, 32))),
        "grad_out": normal_values(key_of[3], (VIDEOS, SEQ, HEADS * HEAD_DIM), 1.0, 6.0, ((0, 8), (1, 32))),
        "q_gain": draw_q_gain(jax.random.fold_in(key_of[7], 71), 0),
        "k_gain": draw_k_gain(jax.random.fold_in(key_of[7], 71), 0),
        "block_masks": draw_block_masks(jax.random.fold_in(key_of[7], 71), 0),
    }


norm_eps = 1e-06
neg_fill = -1e+30

def rms_norm(raw, gain):
    raw_float = raw.astype(jnp.float32)
    spread = jnp.sqrt(lax.optimization_barrier(jnp.mean(raw_float * raw_float, axis=-1, keepdims=True)) + norm_eps)
    return (raw_float, spread, (raw_float / spread * gain).astype(jnp.bfloat16))

def norm_back(raw_float, spread, gain, grad_normed):
    inner = lax.optimization_barrier(jnp.sum(gain * grad_normed * raw_float, axis=-1, keepdims=True))
    return gain * grad_normed / spread - raw_float * inner / (HEAD_DIM * spread ** 3)

def one_head(operands, q_gain, k_gain):
    q_head, k_head, v_head, out_head, mask_head = operands
    q_float, q_spread, q_normed = rms_norm(q_head, q_gain)
    k_float, k_spread, k_normed = rms_norm(k_head, k_gain)
    allowed = jnp.repeat(jnp.repeat(mask_head, BLOCK, 0), BLOCK, 1) > 0
    score_scale = HEAD_DIM ** (-0.5)
    scores = jnp.dot(q_normed, k_normed.T, preferred_element_type=jnp.float32) * score_scale
    scores = jnp.where(allowed, scores, neg_fill)
    peak = lax.optimization_barrier(jnp.max(scores, axis=1, keepdims=True))
    weights = jnp.where(allowed, jnp.exp(scores - peak), 0.0)
    weights = weights / lax.optimization_barrier(jnp.sum(weights, axis=1, keepdims=True))
    grad_weights = jnp.dot(out_head, v_head.T, preferred_element_type=jnp.float32)
    row_delta = lax.optimization_barrier(jnp.sum(weights * grad_weights, axis=1, keepdims=True))
    grad_scores = weights * (grad_weights - row_delta)
    weights_half = weights.astype(jnp.bfloat16)
    scores_half = grad_scores.astype(jnp.bfloat16)
    grad_v = jnp.dot(weights_half.T, out_head, preferred_element_type=jnp.float32)
    grad_qn = jnp.dot(scores_half, k_normed, preferred_element_type=jnp.float32) * score_scale
    grad_kn = jnp.dot(scores_half.T, q_normed, preferred_element_type=jnp.float32) * score_scale
    grad_q = norm_back(q_float, q_spread, q_gain, grad_qn)
    grad_k = norm_back(k_float, k_spread, k_gain, grad_kn)
    gain_q = lax.optimization_barrier(jnp.sum(grad_qn * q_float / q_spread, axis=0))
    gain_k = lax.optimization_barrier(jnp.sum(grad_kn * k_float / k_spread, axis=0))
    return (grad_q, grad_k, grad_v, jnp.stack([gain_q, gain_k]))

def split_heads(array):
    return array.reshape(SEQ, HEADS, HEAD_DIM).transpose(1, 0, 2)

def join_heads(array):
    return array.transpose(1, 0, 2).reshape(SEQ, HEADS * HEAD_DIM).astype(jnp.bfloat16)

def reference(q_raw, k_raw, values, grad_out, q_gain, k_gain, block_masks):
    grads_q = []
    grads_k = []
    grads_v = []
    gain_total = jnp.zeros((2, HEAD_DIM), jnp.float32)
    for video_index in range(VIDEOS):
        operands = (split_heads(q_raw[video_index]), split_heads(k_raw[video_index]), split_heads(values[video_index]), split_heads(grad_out[video_index]), block_masks)
        grad_q, grad_k, grad_v, gain_parts = lax.map(lambda ops: one_head(ops, q_gain, k_gain), operands)
        grads_q.append(join_heads(grad_q))
        grads_k.append(join_heads(grad_k))
        grads_v.append(join_heads(grad_v))
        gain_total = gain_total + lax.optimization_barrier(jnp.sum(gain_parts, axis=0))
    gain_grads = gain_total * (VIDEOS * SEQ * HEADS) ** (-0.5)
    return (jnp.stack(grads_q), jnp.stack(grads_k), jnp.stack(grads_v), gain_grads)
```

```python
import functools

import jax
import jax.numpy as jnp
from jax import lax
from jax.experimental import pallas as pl
from jax.experimental.pallas import tpu as pltpu
from jax.sharding import PartitionSpec as P

HEADS = 24
HEAD_DIM = 128
SPLITS = 8
BLOCK = 128
ITEMS = 32
GROUP = 8

NORM_EPS = 1e-06
NEG_FILL = -1e30
SCALE = HEAD_DIM ** (-0.5)
LOG2E = 1.4426950408889634
SCORE2 = SCALE * LOG2E
SAFE_BOUND = 80.0
F32 = jnp.float32
BF16 = jnp.bfloat16


def pack_kernel(heads_ref, q_ref, k_ref, v_ref, o_ref, out_ref):
    def move(slot, carry):
        at = pl.multiple_of(heads_ref[slot] * HEAD_DIM, HEAD_DIM)
        for which, src in enumerate((q_ref, k_ref, v_ref, o_ref)):
            out_ref[slot, which] = src[:, pl.ds(at, HEAD_DIM)]
        return carry

    lax.fori_loop(0, ITEMS, move, 0)


def pack(item_heads, q_raw, k_raw, values, grad_out):
    rows = q_raw.shape[0]
    vmem = pl.BlockSpec(memory_space=pltpu.VMEM)
    return pl.pallas_call(
        pack_kernel,
        out_shape=jax.ShapeDtypeStruct((ITEMS, 4, rows, HEAD_DIM), BF16),
        in_specs=[pl.BlockSpec(memory_space=pltpu.SMEM)] + [vmem] * 4,
        out_specs=vmem,
        compiler_params=pltpu.CompilerParams(vmem_limit_bytes=24 * 2**20),
        name="pack_heads",
    )(item_heads, q_raw, k_raw, values, grad_out)


def inv_spread(raw_float):
    return lax.rsqrt(jnp.mean(raw_float * raw_float, axis=-1, keepdims=True) + NORM_EPS)


def norm_back(raw_float, gain, grad_normed):
    inv = inv_spread(raw_float)
    unit = raw_float * inv
    scaled = gain * grad_normed
    inner = jnp.sum(scaled * unit, axis=-1, keepdims=True) * (1.0 / HEAD_DIM)
    return (scaled - unit * inner) * inv, grad_normed * unit


def fold_rows(full):
    return jnp.sum(full.reshape(-1, 8, full.shape[-1]), axis=0)


def item_kernel(
    nb, info_ref, list_ref, gain_ref, in_ref, out_ref, part_ref,
    kv, kt, probs, dprobs, acc, left, right, sums,
):
    first, last, careful = info_ref[0], info_ref[1], info_ref[2]
    q_gain = gain_ref[0:1, :]
    k_gain = gain_ref[1:2, :]
    slots = list_ref.shape[0] // nb

    def prepare(j, carry):
        raw = in_ref[j, 1].astype(F32)
        normed = (raw * inv_spread(raw) * k_gain).astype(BF16)
        kv[j, :, :HEAD_DIM] = normed
        kv[j, :, HEAD_DIM:] = in_ref[j, 2]
        kt[j] = normed.T
        acc[j] = jnp.zeros((BLOCK, 2 * HEAD_DIM), F32)
        out_ref[j, 0] = jnp.zeros((BLOCK, HEAD_DIM), BF16)
        return carry

    lax.fori_loop(0, nb, prepare, 0)
    kv[nb] = jnp.zeros((BLOCK, 2 * HEAD_DIM), BF16)
    kt[nb] = jnp.zeros((HEAD_DIM, BLOCK), BF16)
    acc[nb] = jnp.zeros((BLOCK, 2 * HEAD_DIM), F32)
    left[...] = jnp.zeros((2 * HEAD_DIM, 2 * BLOCK), BF16)
    right[...] = jnp.zeros((2 * BLOCK, 2 * HEAD_DIM), BF16)
    part_ref[...] = jnp.zeros((16, HEAD_DIM), F32)

    def query_block(i, carry):
        raw = in_ref[i, 0].astype(F32)
        normed = (raw * inv_spread(raw) * q_gain).astype(BF16)
        o_block = in_ref[i, 3]
        left[:HEAD_DIM, :BLOCK] = normed.T
        left[HEAD_DIM:, BLOCK:] = o_block.T
        right[:BLOCK, :HEAD_DIM] = o_block
        right[BLOCK:, HEAD_DIM:] = normed
        base = i * slots
        count = info_ref[8 + i]
        groups = (count + (GROUP - 1)) // GROUP

        def bias_of(at):
            return jnp.where(at < count, 0.0, NEG_FILL)

        sums[0:1, :] = jnp.zeros((1, BLOCK), F32)

        @pl.when(careful > 0)
        def _():
            def peak_step(at, peak):
                j = list_ref[base + at]
                scores = jnp.dot(kv[j, :, :HEAD_DIM], left[:HEAD_DIM, :BLOCK], preferred_element_type=F32)
                return jnp.maximum(peak, jnp.max(scores.reshape(-1, 8, BLOCK), axis=0))

            peak = lax.fori_loop(0, count, peak_step, jnp.full((8, BLOCK), NEG_FILL, F32))
            sums[0:1, :] = jnp.max(peak, axis=0, keepdims=True) * SCORE2

        shift = sums[0:1, :]

        def score_step(g, stats):
            total, dotted = stats
            at = g * GROUP
            js = [list_ref[base + at + u] for u in range(GROUP)]
            for u in range(GROUP):
                both = jnp.dot(kv[js[u]], left[...], preferred_element_type=F32)
                weights = jnp.exp2(both[:, :BLOCK] * SCORE2 + (bias_of(at + u) - shift))
                grads = both[:, BLOCK:]
                probs[at + u] = weights
                dprobs[at + u] = grads
                total = total + fold_rows(weights)
                dotted = dotted + fold_rows(weights * grads)
            return total, dotted

        zero = jnp.zeros((8, BLOCK), F32)
        total, dotted = lax.fori_loop(0, groups, score_step, (zero, zero))
        inv_total = 1.0 / jnp.sum(total, axis=0, keepdims=True)
        row_delta = jnp.sum(dotted, axis=0, keepdims=True) * inv_total

        def grad_step(g, grad_qt):
            at = g * GROUP
            js = [list_ref[base + at + u] for u in range(GROUP)]
            s_parts = []
            for u in range(GROUP):
                weights = probs[at + u] * inv_total
                scores = (weights * (dprobs[at + u] - row_delta)).astype(BF16)
                s_parts.append(scores)
                acc[js[u]] += jnp.dot(
                    jnp.concatenate([weights.astype(BF16), scores], axis=1), right[...], preferred_element_type=F32
                )
            scores_half = jnp.concatenate(s_parts, axis=0)
            keys_t = jnp.concatenate([kt[j] for j in js], axis=1)
            return grad_qt + jnp.dot(keys_t, scores_half, preferred_element_type=F32)

        grad_qt = lax.fori_loop(0, groups, grad_step, jnp.zeros((HEAD_DIM, BLOCK), F32))
        grad, gains = norm_back(raw, q_gain, grad_qt.T * SCALE)
        out_ref[i, 0] = grad.astype(BF16)
        part_ref[0:8, :] += fold_rows(gains)
        return carry

    lax.fori_loop(first, last, query_block, 0)

    def finish(j, carry):
        grad, gains = norm_back(in_ref[j, 1].astype(F32), k_gain, acc[j, :, HEAD_DIM:] * SCALE)
        out_ref[j, 1] = grad.astype(BF16)
        out_ref[j, 2] = acc[j, :, :HEAD_DIM].astype(BF16)
        part_ref[8:16, :] += fold_rows(gains)
        return carry

    lax.fori_loop(0, nb, finish, 0)


def item_grads(info, block_list, gains, arrived):
    nb = arrived.shape[0]
    slots = block_list.shape[0] // nb
    smem = pl.BlockSpec(memory_space=pltpu.SMEM)
    vmem = pl.BlockSpec(memory_space=pltpu.VMEM)
    return pl.pallas_call(
        functools.partial(item_kernel, nb),
        out_shape=(
            jax.ShapeDtypeStruct((nb, 3, BLOCK, HEAD_DIM), BF16),
            jax.ShapeDtypeStruct((16, HEAD_DIM), F32),
        ),
        in_specs=[smem, smem, vmem, vmem],
        out_specs=(vmem, vmem),
        scratch_shapes=[
            pltpu.VMEM((nb + 1, BLOCK, 2 * HEAD_DIM), BF16),
            pltpu.VMEM((nb + 1, HEAD_DIM, BLOCK), BF16),
            pltpu.VMEM((slots, BLOCK, BLOCK), F32),
            pltpu.VMEM((slots, BLOCK, BLOCK), F32),
            pltpu.VMEM((nb + 1, BLOCK, 2 * HEAD_DIM), F32),
            pltpu.VMEM((2 * HEAD_DIM, 2 * BLOCK), BF16),
            pltpu.VMEM((2 * BLOCK, 2 * HEAD_DIM), BF16),
            pltpu.VMEM((8, BLOCK), F32),
        ],
        compiler_params=pltpu.CompilerParams(vmem_limit_bytes=40 * 2**20),
        name="item_grads",
    )(info, block_list, gains, arrived)


def merge_kernel(heads_ref, in_ref, q_ref, k_ref, v_ref):
    outs = (q_ref, k_ref, v_ref)

    def pair(p, carry):
        at = pl.multiple_of(heads_ref[2 * p] * HEAD_DIM, HEAD_DIM)
        for which, out in enumerate(outs):
            both = in_ref[2 * p, which].astype(F32) + in_ref[2 * p + 1, which].astype(F32)
            out[:, pl.ds(at, HEAD_DIM)] = both.astype(BF16)
        return carry

    def single(slot, carry):
        at = pl.multiple_of(heads_ref[slot] * HEAD_DIM, HEAD_DIM)
        for which, out in enumerate(outs):
            out[:, pl.ds(at, HEAD_DIM)] = in_ref[slot, which]
        return carry

    lax.fori_loop(0, SPLITS, pair, 0)
    lax.fori_loop(2 * SPLITS, ITEMS, single, 0)


def merge(item_heads, returned):
    rows = returned.shape[2]
    vmem = pl.BlockSpec(memory_space=pltpu.VMEM)
    wide = jax.ShapeDtypeStruct((rows, HEADS * HEAD_DIM), BF16)
    return pl.pallas_call(
        merge_kernel,
        out_shape=(wide, wide, wide),
        in_specs=[pl.BlockSpec(memory_space=pltpu.SMEM), vmem],
        out_specs=(vmem, vmem, vmem),
        compiler_params=pltpu.CompilerParams(vmem_limit_bytes=24 * 2**20),
        name="merge_heads",
    )(item_heads, returned)


def plan_items(block_masks):
    totals = jnp.sum((block_masks > 0).astype(jnp.int32), axis=(1, 2))
    heads = jnp.arange(HEADS, dtype=jnp.int32)
    ahead = (totals[None, :] > totals[:, None]) | (
        (totals[None, :] == totals[:, None]) & (heads[None, :] < heads[:, None])
    )
    rank = jnp.sum(ahead.astype(jnp.int32), axis=1)
    counter = jnp.arange(ITEMS, dtype=jnp.int32)
    wanted = jnp.where(counter < 2 * SPLITS, counter // 2, counter - SPLITS)
    return jnp.sum(jnp.where(rank[None, :] == wanted[:, None], heads[None, :], 0), axis=1)


def block_lists(mask_head):
    nb = mask_head.shape[0]
    on = (mask_head > 0).astype(jnp.int32)
    lower = (jnp.arange(nb)[:, None] < jnp.arange(nb)[None, :]).astype(jnp.int32)
    place = jnp.sum(on[:, :, None] * lower[None, :, :], axis=1)
    slot = jnp.arange(nb + GROUP, dtype=jnp.int32)
    hit = (on[:, :, None] > 0) & (place[:, :, None] == slot[None, None, :])
    which = jnp.arange(nb, dtype=jnp.int32)[None, :, None]
    counts = jnp.sum(on, axis=1)
    lists = nb + jnp.sum(jnp.where(hit, which - nb, 0), axis=1)
    return counts, lists


def body(q_raw, k_raw, values, grad_out, q_gain, k_gain, block_masks):
    device_rank = lax.axis_index("ulysses")
    tok_rows, width = q_raw.shape[1:]
    nb = block_masks.shape[1]
    seq_len = tok_rows * lax.axis_size("ulysses")
    videos = lax.axis_size("dp")
    item_heads = plan_items(block_masks)
    outgoing = pack(item_heads, q_raw[0], k_raw[0], values[0], grad_out[0])
    arrived = lax.all_to_all(outgoing, "ulysses", split_axis=0, concat_axis=0, tiled=True)
    head = lax.dynamic_index_in_dim(item_heads, device_rank, 0, keepdims=False)
    counts, lists = block_lists(lax.dynamic_index_in_dim(block_masks, head, 0, keepdims=False))
    split = device_rank < 2 * SPLITS
    half = device_rank % 2
    first = jnp.where(split, half * (nb // 2), 0)
    last = jnp.where(split, (half + 1) * (nb // 2), nb)
    bound = 1.02 * HEAD_DIM * SCORE2 * jnp.max(jnp.abs(q_gain)) * jnp.max(jnp.abs(k_gain))
    careful = jnp.where(bound < SAFE_BOUND, 0, 1)
    info = jnp.concatenate(
        [jnp.stack([first, last, careful]).astype(jnp.int32), jnp.zeros((5,), jnp.int32), counts]
    )
    gains = jnp.stack([q_gain, k_gain])
    grads, part = item_grads(info, lists.reshape(-1), gains, arrived)
    returned = lax.all_to_all(grads, "ulysses", split_axis=0, concat_axis=0, tiled=True)
    summed = lax.psum(jnp.sum(part.reshape(2, 8, HEAD_DIM), axis=1), ("dp", "ulysses"))
    grad_q, grad_k, grad_v = merge(item_heads, returned)
    gain_grads = summed * (videos * seq_len * HEADS) ** (-0.5)
    return (grad_q[None], grad_k[None], grad_v[None], gain_grads)


def solution(mesh):
    tokens = P("dp", "ulysses", None)
    return jax.shard_map(
        body,
        mesh=mesh,
        in_specs=(tokens, tokens, tokens, tokens, P(), P(), P()),
        out_specs=(tokens, tokens, tokens, P()),
        check_vma=False,
    )
```

```python
import functools

import jax
import jax.numpy as jnp
from jax import lax
from jax.experimental import pallas as pl
from jax.experimental.pallas import tpu as pltpu
from jax.sharding import PartitionSpec as P

HEADS = 24
HEAD_DIM = 128
SPLITS = 8
BLOCK = 128
ITEMS = 32
DENSE_GROUP = 16
SPARSE_GROUP = 4
DENSE_FROM = 12
CHUNK = 4
UNROLL = 4

NORM_EPS = 1e-06
NEG_FILL = -1e30
SCALE = HEAD_DIM ** (-0.5)
LOG2E = 1.4426950408889634
SCORE2 = SCALE * LOG2E
SAFE_BOUND = 50.0
F32 = jnp.float32
BF16 = jnp.bfloat16


def pack_kernel(heads_ref, q_ref, k_ref, v_ref, o_ref, out_ref, wide, tall, in_sems, out_sems):
    rows = q_ref.shape[0]
    part = rows // CHUNK
    loads, stores = [], []
    for which, src in enumerate((q_ref, k_ref, v_ref, o_ref)):
        for c in range(CHUNK):
            at = pl.ds(c * part, part)
            copy = pltpu.make_async_copy(src.at[at], wide.at[which, at], in_sems.at[which, c])
            copy.start()
            loads.append(copy)
    for which in range(4):
        for c in range(CHUNK):
            loads[which * CHUNK + c].wait()

        def move(slot, carry, which=which):
            at = pl.multiple_of(heads_ref[slot] * HEAD_DIM, HEAD_DIM)
            tall[which, slot] = wide[which, :, pl.ds(at, HEAD_DIM)]
            return carry

        lax.fori_loop(0, ITEMS, move, 0)
        copy = pltpu.make_async_copy(tall.at[which], out_ref.at[:, which], out_sems.at[which])
        copy.start()
        stores.append(copy)
    for copy in stores:
        copy.wait()


def pack(item_heads, q_raw, k_raw, values, grad_out):
    rows, width = q_raw.shape
    hbm = pl.BlockSpec(memory_space=pltpu.HBM)
    return pl.pallas_call(
        pack_kernel,
        out_shape=jax.ShapeDtypeStruct((ITEMS, 4, rows, HEAD_DIM), BF16),
        in_specs=[pl.BlockSpec(memory_space=pltpu.SMEM)] + [hbm] * 4,
        out_specs=hbm,
        scratch_shapes=[
            pltpu.VMEM((4, rows, width), BF16),
            pltpu.VMEM((4, ITEMS, rows, HEAD_DIM), BF16),
            pltpu.SemaphoreType.DMA((4, CHUNK)),
            pltpu.SemaphoreType.DMA((4,)),
        ],
        compiler_params=pltpu.CompilerParams(vmem_limit_bytes=60 * 2**20),
        name="pack_heads",
    )(item_heads, q_raw, k_raw, values, grad_out)


def inv_spread(raw_float):
    return lax.rsqrt(jnp.mean(raw_float * raw_float, axis=-1, keepdims=True) + NORM_EPS)


def norm_back(raw_float, gain, grad_normed):
    inv = inv_spread(raw_float)
    unit = raw_float * inv
    scaled = gain * grad_normed
    inner = jnp.sum(scaled * unit, axis=-1, keepdims=True) * (1.0 / HEAD_DIM)
    return (scaled - unit * inner) * inv, grad_normed * unit


def fold_rows(full):
    return jnp.sum(full.reshape(-1, 8, full.shape[-1]), axis=0)


def item_kernel(
    nb, info_ref, list_ref, gain_ref, hbm_ref, qk_ref, v_ref, part_ref,
    in_ref, qk_out, v_out, in_sems, qk_sems, v_sems, kv, kt, pairs_even, pairs_odd, acc, left, right, grad_qt, shifts,
):
    first, last, careful = info_ref[0], info_ref[1], info_ref[2]
    q_gain = gain_ref[0:1, :]
    k_gain = gain_ref[1:2, :]
    slots = list_ref.shape[0] // nb
    zero_half = jnp.zeros((BLOCK, HEAD_DIM), BF16)

    def load(step):
        at = pl.ds(step * UNROLL, UNROLL)
        return pltpu.make_async_copy(hbm_ref.at[at], in_ref.at[at], in_sems.at[step])

    def store(step):
        at = pl.ds(step * UNROLL, UNROLL)
        return (
            pltpu.make_async_copy(qk_out.at[at], qk_ref.at[at], qk_sems.at[step]),
            pltpu.make_async_copy(v_out.at[at], v_ref.at[at], v_sems.at[step]),
        )

    for step in range(nb // UNROLL):
        load(step).start()

    def prepare_keys(step, carry):
        load(step).wait()
        for u in range(UNROLL):
            j = step * UNROLL + u
            raw = in_ref[j, 1].astype(F32)
            normed = (raw * inv_spread(raw) * k_gain).astype(BF16)
            kv[j, :, :HEAD_DIM] = normed
            kv[j, :, HEAD_DIM:] = in_ref[j, 2]
            kt[j] = normed.T
            acc[j] = jnp.zeros((BLOCK, 2 * HEAD_DIM), F32)
            qk_out[j, 0] = zero_half
        return carry

    def prepare_queries(step, carry):
        for u in range(UNROLL):
            i = first + step * UNROLL + u
            raw = in_ref[i, 0].astype(F32)
            normed = (raw * inv_spread(raw) * q_gain).astype(BF16)
            o_block = in_ref[i, 3]
            left[i, :HEAD_DIM, :BLOCK] = normed.T
            left[i, HEAD_DIM:, BLOCK:] = o_block.T
            left[i, :HEAD_DIM, BLOCK:] = zero_half
            left[i, HEAD_DIM:, :BLOCK] = zero_half
            right[i, :BLOCK, :HEAD_DIM] = o_block
            right[i, BLOCK:, HEAD_DIM:] = normed
            right[i, :BLOCK, HEAD_DIM:] = zero_half
            right[i, BLOCK:, :HEAD_DIM] = zero_half
            shifts[i] = jnp.zeros((8, BLOCK), F32)
        return carry

    lax.fori_loop(0, nb // UNROLL, prepare_keys, 0)
    lax.fori_loop(0, (last - first) // UNROLL, prepare_queries, 0)
    kv[nb] = jnp.zeros((BLOCK, 2 * HEAD_DIM), BF16)
    kt[nb] = zero_half
    acc[nb] = jnp.zeros((BLOCK, 2 * HEAD_DIM), F32)

    def clear(at, carry):
        pairs_even[at] = jnp.zeros((BLOCK, 2 * BLOCK), F32)
        pairs_odd[at] = jnp.zeros((BLOCK, 2 * BLOCK), F32)
        return carry

    lax.fori_loop(0, slots, clear, 0)
    part_ref[...] = jnp.zeros((16, HEAD_DIM), F32)

    @pl.when(careful > 0)
    def _():
        def peak_row(i, carry):
            def peak_step(at, peak):
                j = list_ref[i * slots + at]
                scores = jnp.dot(kv[j, :, :HEAD_DIM], left[i, :HEAD_DIM, :BLOCK], preferred_element_type=F32)
                return jnp.maximum(peak, jnp.max(scores.reshape(-1, 8, BLOCK), axis=0))

            peak = lax.fori_loop(0, info_ref[8 + i], peak_step, jnp.full((8, BLOCK), NEG_FILL, F32))
            shifts[i] = jnp.broadcast_to(jnp.max(peak, axis=0, keepdims=True) * SCORE2, (8, BLOCK))
            return carry

        lax.fori_loop(first, last, peak_row, 0)

    def groups_of(i, size):
        return (info_ref[8 + i] + (size - 1)) // size

    def score_group(size, pairs, i, g, stats):
        total, dotted = stats
        count = info_ref[8 + i]
        shift = shifts[i, 0:1, :]
        for u in range(size):
            at = g * size + u
            both = jnp.dot(kv[list_ref[i * slots + at]], left[i], preferred_element_type=F32)
            weights = jnp.exp2(both[:, :BLOCK] * SCORE2 + (jnp.where(at < count, 0.0, NEG_FILL) - shift))
            grads = both[:, BLOCK:]
            pairs[at, :, :BLOCK] = weights
            pairs[at, :, BLOCK:] = grads
            total = total + fold_rows(weights)
            dotted = dotted + fold_rows(weights * grads)
        return total, dotted

    def grad_group(size, pairs, i, g, inv_total, row_delta, total_qt):
        halves, keys = [], []
        for u in range(size):
            at = g * size + u
            j = list_ref[i * slots + at]
            weights = pairs[at, :, :BLOCK] * inv_total
            half = (weights * (pairs[at, :, BLOCK:] - row_delta)).astype(BF16)
            acc[j] += jnp.dot(
                jnp.concatenate([weights.astype(BF16), half], axis=1), right[i], preferred_element_type=F32
            )
            halves.append(half)
            keys.append(kt[j])
        return total_qt + jnp.dot(
            jnp.concatenate(keys, axis=1), jnp.concatenate(halves, axis=0), preferred_element_type=F32
        )

    zero = jnp.zeros((8, BLOCK), F32)
    def attend(size):
        stats = lax.fori_loop(
            0, groups_of(first, size), lambda g, s: score_group(size, pairs_even, first, g, s), (zero, zero)
        )

        def query_block(i, later, mine, other, stats):
            total, dotted = stats
            inv_total = 1.0 / jnp.sum(total, axis=0, keepdims=True)
            row_delta = jnp.sum(dotted, axis=0, keepdims=True) * inv_total

            def step(g, carry):
                total_qt, total, dotted = carry
                total_qt = grad_group(size, mine, i, g, inv_total, row_delta, total_qt)
                total, dotted = score_group(size, other, later, g, (total, dotted))
                return total_qt, total, dotted

            total_qt, total, dotted = lax.fori_loop(
                0,
                jnp.maximum(groups_of(i, size), groups_of(later, size)),
                step,
                (jnp.zeros((HEAD_DIM, BLOCK), F32), zero, zero),
            )
            grad_qt[i] = total_qt
            return total, dotted

        def two_blocks(step, stats):
            i = first + 2 * step
            stats = query_block(i, i + 1, pairs_even, pairs_odd, stats)
            return query_block(i + 1, jnp.minimum(i + 2, last - 1), pairs_odd, pairs_even, stats)

        lax.fori_loop(0, (last - first) // 2, two_blocks, stats)

    dense = info_ref[3]
    pl.when(dense > 0)(lambda: attend(DENSE_GROUP))
    pl.when(dense == 0)(lambda: attend(SPARSE_GROUP))

    def finish_queries(step, total):
        for u in range(UNROLL):
            i = first + step * UNROLL + u
            grad, gains = norm_back(in_ref[i, 0].astype(F32), q_gain, grad_qt[i].T * SCALE)
            qk_out[i, 0] = grad.astype(BF16)
            total = total + fold_rows(gains)
        return total

    def finish_keys(step, total):
        for u in range(UNROLL):
            j = step * UNROLL + u
            grad, gains = norm_back(in_ref[j, 1].astype(F32), k_gain, acc[j, :, HEAD_DIM:] * SCALE)
            qk_out[j, 1] = grad.astype(BF16)
            v_out[j] = acc[j, :, :HEAD_DIM].astype(BF16)
            total = total + fold_rows(gains)
        for copy in store(step):
            copy.start()
        return total

    part_ref[0:8, :] = lax.fori_loop(0, (last - first) // UNROLL, finish_queries, zero)
    part_ref[8:16, :] = lax.fori_loop(0, nb // UNROLL, finish_keys, zero)
    for step in range(nb // UNROLL):
        for copy in store(step):
            copy.wait()


def item_grads(info, block_list, gains, arrived):
    nb = arrived.shape[0]
    slots = block_list.shape[0] // nb
    smem = pl.BlockSpec(memory_space=pltpu.SMEM)
    vmem = pl.BlockSpec(memory_space=pltpu.VMEM)
    hbm = pl.BlockSpec(memory_space=pltpu.HBM)
    return pl.pallas_call(
        functools.partial(item_kernel, nb),
        out_shape=(
            jax.ShapeDtypeStruct((nb, 2, BLOCK, HEAD_DIM), BF16),
            jax.ShapeDtypeStruct((nb, BLOCK, HEAD_DIM), BF16),
            jax.ShapeDtypeStruct((16, HEAD_DIM), F32),
        ),
        in_specs=[smem, smem, vmem, hbm],
        out_specs=(hbm, hbm, vmem),
        scratch_shapes=[
            pltpu.VMEM((nb, 4, BLOCK, HEAD_DIM), BF16),
            pltpu.VMEM((nb, 2, BLOCK, HEAD_DIM), BF16),
            pltpu.VMEM((nb, BLOCK, HEAD_DIM), BF16),
            pltpu.SemaphoreType.DMA((nb // UNROLL,)),
            pltpu.SemaphoreType.DMA((nb // UNROLL,)),
            pltpu.SemaphoreType.DMA((nb // UNROLL,)),
            pltpu.VMEM((nb + 1, BLOCK, 2 * HEAD_DIM), BF16),
            pltpu.VMEM((nb + 1, HEAD_DIM, BLOCK), BF16),
            pltpu.VMEM((slots, BLOCK, 2 * BLOCK), F32),
            pltpu.VMEM((slots, BLOCK, 2 * BLOCK), F32),
            pltpu.VMEM((nb + 1, BLOCK, 2 * HEAD_DIM), F32),
            pltpu.VMEM((nb, 2 * HEAD_DIM, 2 * BLOCK), BF16),
            pltpu.VMEM((nb, 2 * BLOCK, 2 * HEAD_DIM), BF16),
            pltpu.VMEM((nb, HEAD_DIM, BLOCK), F32),
            pltpu.VMEM((nb, 8, BLOCK), F32),
        ],
        compiler_params=pltpu.CompilerParams(vmem_limit_bytes=60 * 2**20),
        name="item_grads",
    )(info, block_list, gains, arrived)


def merge_kernel(count, heads_ref, in_ref, *out_refs):
    outs = out_refs[:count]

    def piece(slot, which):
        return in_ref[slot, which * BLOCK : (which + 1) * BLOCK, :]

    def pair(p, carry):
        at = pl.multiple_of(heads_ref[2 * p] * HEAD_DIM, HEAD_DIM)
        for which, out in enumerate(outs):
            both = piece(2 * p, which).astype(F32) + piece(2 * p + 1, which).astype(F32)
            out[:, pl.ds(at, HEAD_DIM)] = both.astype(BF16)
        return carry

    def single(slot, carry):
        at = pl.multiple_of(heads_ref[slot] * HEAD_DIM, HEAD_DIM)
        for which, out in enumerate(outs):
            out[:, pl.ds(at, HEAD_DIM)] = piece(slot, which)
        return carry

    lax.fori_loop(0, SPLITS, pair, 0)
    lax.fori_loop(2 * SPLITS, ITEMS, single, 0)
    if len(out_refs) > count:
        def tail(slot, total):
            return total + in_ref[slot, count * BLOCK : count * BLOCK + 16, :].astype(F32)

        total = lax.fori_loop(0, ITEMS, tail, jnp.zeros((16, HEAD_DIM), F32))
        out_refs[count][...] = total[0:2] + (total[2:4] + total[4:6])


def merge(item_heads, returned, count, with_tail):
    vmem = pl.BlockSpec(memory_space=pltpu.VMEM)
    wide = jax.ShapeDtypeStruct((BLOCK, HEADS * HEAD_DIM), BF16)
    shapes = (wide,) * count + ((jax.ShapeDtypeStruct((2, HEAD_DIM), F32),) if with_tail else ())
    return pl.pallas_call(
        functools.partial(merge_kernel, count),
        out_shape=shapes,
        in_specs=[pl.BlockSpec(memory_space=pltpu.SMEM), vmem],
        out_specs=(vmem,) * len(shapes),
        compiler_params=pltpu.CompilerParams(vmem_limit_bytes=24 * 2**20),
        name="merge_heads",
    )(item_heads, returned)


def attach_kernel(part_ref, v_ref, out_ref):
    total = part_ref[...]
    high = total.astype(BF16)
    rest = total - high.astype(F32)
    middle = rest.astype(BF16)
    low = (rest - middle.astype(F32)).astype(BF16)
    pieces = [high.astype(F32), middle.astype(F32), low.astype(F32), jnp.zeros((10, HEAD_DIM), F32)]
    tail = jnp.concatenate(pieces, axis=0).astype(BF16)

    def move(slot, carry):
        out_ref[slot, :BLOCK, :] = v_ref[slot]
        out_ref[slot, BLOCK:, :] = tail
        return carry

    lax.fori_loop(0, ITEMS, move, 0)


def attach(part, grads_v):
    vmem = pl.BlockSpec(memory_space=pltpu.VMEM)
    return pl.pallas_call(
        attach_kernel,
        out_shape=jax.ShapeDtypeStruct((ITEMS, BLOCK + 16, HEAD_DIM), BF16),
        in_specs=[vmem, vmem],
        out_specs=vmem,
        name="attach_gains",
    )(part, grads_v)


def sum_over_videos(part):
    count = lax.axis_size("dp")
    step = 1
    while step < count:
        part = part + lax.ppermute(part, "dp", [(i, i ^ step) for i in range(count)])
        step *= 2
    return part


def plan_items(block_masks):
    totals = jnp.sum((block_masks > 0).astype(jnp.int32), axis=(1, 2))
    heads = jnp.arange(HEADS, dtype=jnp.int32)
    ahead = (totals[None, :] > totals[:, None]) | (
        (totals[None, :] == totals[:, None]) & (heads[None, :] < heads[:, None])
    )
    rank = jnp.sum(ahead.astype(jnp.int32), axis=1)
    counter = jnp.arange(ITEMS, dtype=jnp.int32)
    wanted = jnp.where(counter < 2 * SPLITS, counter // 2, counter - SPLITS)
    return jnp.sum(jnp.where(rank[None, :] == wanted[:, None], heads[None, :], 0), axis=1)


def block_lists(mask_head):
    nb = mask_head.shape[0]
    on = (mask_head > 0).astype(jnp.int32)
    lower = (jnp.arange(nb)[:, None] < jnp.arange(nb)[None, :]).astype(jnp.int32)
    place = jnp.sum(on[:, :, None] * lower[None, :, :], axis=1)
    slot = jnp.arange(nb, dtype=jnp.int32)
    hit = (on[:, :, None] > 0) & (place[:, :, None] == slot[None, None, :])
    which = jnp.arange(nb, dtype=jnp.int32)[None, :, None]
    counts = jnp.sum(on, axis=1)
    lists = nb + jnp.sum(jnp.where(hit, which - nb, 0), axis=1)
    return counts, lists


def body(q_raw, k_raw, values, grad_out, q_gain, k_gain, block_masks):
    device_rank = lax.axis_index("ulysses")
    tok_rows, width = q_raw.shape[1:]
    nb = block_masks.shape[1]
    seq_len = tok_rows * lax.axis_size("ulysses")
    videos = lax.axis_size("dp")
    item_heads = plan_items(block_masks)
    outgoing = pack(item_heads, q_raw[0], k_raw[0], values[0], grad_out[0])
    arrived = lax.all_to_all(outgoing, "ulysses", split_axis=0, concat_axis=0, tiled=True)
    head = lax.dynamic_index_in_dim(item_heads, device_rank, 0, keepdims=False)
    counts, lists = block_lists(lax.dynamic_index_in_dim(block_masks, head, 0, keepdims=False))
    split = device_rank < 2 * SPLITS
    half = device_rank % 2
    first = jnp.where(split, half * (nb // 2), 0)
    last = jnp.where(split, (half + 1) * (nb // 2), nb)
    bound = 1.02 * HEAD_DIM * SCORE2 * jnp.max(jnp.abs(q_gain)) * jnp.max(jnp.abs(k_gain))
    careful = jnp.where(bound < SAFE_BOUND, 0, 1)
    dense = jnp.where(jnp.max(counts) > DENSE_FROM, 1, 0)
    info = jnp.concatenate(
        [jnp.stack([first, last, careful, dense]).astype(jnp.int32), jnp.zeros((4,), jnp.int32), counts]
    )
    gains = jnp.stack([q_gain, k_gain])
    grads_qk, grads_v, part = item_grads(info, lists.reshape(-1), gains, arrived)
    back_qk = lax.all_to_all(
        grads_qk.reshape(nb, 2 * BLOCK, HEAD_DIM), "ulysses", split_axis=0, concat_axis=0, tiled=True
    )
    part = sum_over_videos(jnp.sum(part.reshape(2, 8, HEAD_DIM), axis=1))
    attached, back_qk = lax.optimization_barrier((attach(part, grads_v), back_qk))
    back_v = lax.all_to_all(attached, "ulysses", split_axis=0, concat_axis=0, tiled=True)
    grad_q, grad_k = merge(item_heads, back_qk, 2, False)
    grad_v, summed = merge(item_heads, back_v, 1, True)
    gain_grads = summed * (videos * seq_len * HEADS) ** (-0.5)
    return (grad_q[None], grad_k[None], grad_v[None], gain_grads)


def solution(mesh):
    tokens = P("dp", "ulysses", None)
    return jax.shard_map(
        body,
        mesh=mesh,
        in_specs=(tokens, tokens, tokens, tokens, P(), P(), P()),
        out_specs=(tokens, tokens, tokens, P()),
        check_vma=False,
    )
```

```python
import functools

import jax
import jax.numpy as jnp
from jax import lax
from jax.experimental import pallas as pl
from jax.experimental.pallas import tpu as pltpu
from jax.sharding import PartitionSpec as P

HEADS = 24
HEAD_DIM = 128
SPLITS = 8
BLOCK = 128
ITEMS = 32
GROUP = 5
DENSE_FROM = 12
CHUNK = 4
UNROLL = 4

NORM_EPS = 1e-06
NEG_FILL = -1e30
SCALE = HEAD_DIM ** (-0.5)
LOG2E = 1.4426950408889634
SCORE2 = SCALE * LOG2E
SAFE_BOUND = 50.0
F32 = jnp.float32
BF16 = jnp.bfloat16


def pack_kernel(heads_ref, q_ref, k_ref, v_ref, o_ref, out_ref, wide, tall, in_sems, out_sems):
    rows = q_ref.shape[0]
    part = rows // CHUNK
    loads, stores = [], []
    for which, src in enumerate((q_ref, k_ref, v_ref, o_ref)):
        for c in range(CHUNK):
            at = pl.ds(c * part, part)
            copy = pltpu.make_async_copy(src.at[at], wide.at[which, at], in_sems.at[which, c])
            copy.start()
            loads.append(copy)
    for which in range(4):
        for c in range(CHUNK):
            loads[which * CHUNK + c].wait()

        def move(slot, carry, which=which):
            at = pl.multiple_of(heads_ref[slot] * HEAD_DIM, HEAD_DIM)
            tall[which, slot] = wide[which, :, pl.ds(at, HEAD_DIM)]
            return carry

        lax.fori_loop(0, ITEMS, move, 0)
        copy = pltpu.make_async_copy(tall.at[which], out_ref.at[:, which], out_sems.at[which])
        copy.start()
        stores.append(copy)
    for copy in stores:
        copy.wait()


def pack(item_heads, q_raw, k_raw, values, grad_out):
    rows, width = q_raw.shape
    hbm = pl.BlockSpec(memory_space=pltpu.HBM)
    return pl.pallas_call(
        pack_kernel,
        out_shape=jax.ShapeDtypeStruct((ITEMS, 4, rows, HEAD_DIM), BF16),
        in_specs=[pl.BlockSpec(memory_space=pltpu.SMEM)] + [hbm] * 4,
        out_specs=hbm,
        scratch_shapes=[
            pltpu.VMEM((4, rows, width), BF16),
            pltpu.VMEM((4, ITEMS, rows, HEAD_DIM), BF16),
            pltpu.SemaphoreType.DMA((4, CHUNK)),
            pltpu.SemaphoreType.DMA((4,)),
        ],
        compiler_params=pltpu.CompilerParams(vmem_limit_bytes=60 * 2**20),
        name="pack_heads",
    )(item_heads, q_raw, k_raw, values, grad_out)


def inv_spread(raw_float):
    return lax.rsqrt(jnp.mean(raw_float * raw_float, axis=-1, keepdims=True) + NORM_EPS)


def norm_back(raw_float, gain, grad_normed):
    inv = inv_spread(raw_float)
    unit = raw_float * inv
    scaled = gain * grad_normed
    inner = jnp.sum(scaled * unit, axis=-1, keepdims=True) * (1.0 / HEAD_DIM)
    return (scaled - unit * inner) * inv, grad_normed * unit


def fold_rows(full):
    return jnp.sum(full.reshape(-1, 8, full.shape[-1]), axis=0)


def item_kernel(
    nb, info_ref, list_ref, mask_ref, gain_ref, hbm_ref, qk_ref, v_ref, part_ref,
    in_ref, qk_out, v_out, in_sems, qk_sems, v_sems, kv, kt, pairs_even, pairs_odd, acc, left, right, grad_qt, shifts,
):
    first, last, careful = info_ref[0], info_ref[1], info_ref[2]
    q_gain = gain_ref[0:1, :]
    k_gain = gain_ref[1:2, :]
    slots = list_ref.shape[0] // nb
    zero_half = jnp.zeros((BLOCK, HEAD_DIM), BF16)

    def load(step):
        at = pl.ds(step * UNROLL, UNROLL)
        return pltpu.make_async_copy(hbm_ref.at[at], in_ref.at[at], in_sems.at[step])

    def store(step):
        at = pl.ds(step * UNROLL, UNROLL)
        return (
            pltpu.make_async_copy(qk_out.at[at], qk_ref.at[at], qk_sems.at[step]),
            pltpu.make_async_copy(v_out.at[at], v_ref.at[at], v_sems.at[step]),
        )

    for step in range(nb // UNROLL):
        load(step).start()

    def prepare_keys(step, carry):
        load(step).wait()
        for u in range(UNROLL):
            j = step * UNROLL + u
            raw = in_ref[j, 1].astype(F32)
            normed = (raw * inv_spread(raw) * k_gain).astype(BF16)
            kv[j, :, :HEAD_DIM] = normed
            kv[j, :, HEAD_DIM:] = in_ref[j, 2]
            kt[j] = normed.T
            acc[j] = jnp.zeros((BLOCK, 2 * HEAD_DIM), F32)
            qk_out[j, 0] = zero_half
        return carry

    def prepare_queries(step, carry):
        for u in range(UNROLL):
            i = first + step * UNROLL + u
            raw = in_ref[i, 0].astype(F32)
            normed = (raw * inv_spread(raw) * q_gain).astype(BF16)
            o_block = in_ref[i, 3]
            left[i, :HEAD_DIM, :BLOCK] = normed.T
            left[i, HEAD_DIM:, BLOCK:] = o_block.T
            left[i, :HEAD_DIM, BLOCK:] = zero_half
            left[i, HEAD_DIM:, :BLOCK] = zero_half
            right[i, :BLOCK, :HEAD_DIM] = o_block
            right[i, BLOCK:, HEAD_DIM:] = normed
            right[i, :BLOCK, HEAD_DIM:] = zero_half
            right[i, BLOCK:, :HEAD_DIM] = zero_half
            shifts[i] = jnp.zeros((8, BLOCK), F32)
        return carry

    lax.fori_loop(0, nb // UNROLL, prepare_keys, 0)
    lax.fori_loop(0, (last - first) // UNROLL, prepare_queries, 0)
    kv[nb] = jnp.zeros((BLOCK, 2 * HEAD_DIM), BF16)
    kt[nb] = zero_half
    acc[nb] = jnp.zeros((BLOCK, 2 * HEAD_DIM), F32)

    part_ref[...] = jnp.zeros((16, HEAD_DIM), F32)

    @pl.when(careful > 0)
    def _():
        def peak_row(i, carry):
            def peak_step(at, peak):
                j = list_ref[i * slots + at]
                scores = jnp.dot(kv[j, :, :HEAD_DIM], left[i, :HEAD_DIM, :BLOCK], preferred_element_type=F32)
                return jnp.maximum(peak, jnp.max(scores.reshape(-1, 8, BLOCK), axis=0))

            peak = lax.fori_loop(0, info_ref[8 + i], peak_step, jnp.full((8, BLOCK), NEG_FILL, F32))
            shifts[i] = jnp.broadcast_to(jnp.max(peak, axis=0, keepdims=True) * SCORE2, (8, BLOCK))
            return carry

        lax.fori_loop(first, last, peak_row, 0)

    def score_group(pairs, i, places, stats):
        total, dotted = stats
        shift = shifts[i, 0:1, :]
        for at, j, allowed in places:
            both = jnp.dot(kv[j], left[i], preferred_element_type=F32)
            weights = jnp.exp2(both[:, :BLOCK] * SCORE2 + (jnp.where(allowed, 0.0, NEG_FILL) - shift))
            grads = both[:, BLOCK:]
            pairs[at, :, :BLOCK] = weights
            pairs[at, :, BLOCK:] = grads
            total = total + fold_rows(weights)
            dotted = dotted + fold_rows(weights * grads)
        return total, dotted

    def grad_group(pairs, i, places, inv_total, row_delta, total_qt):
        halves, keys = [], []
        for at, j, _ in places:
            weights = pairs[at, :, :BLOCK] * inv_total
            half = (weights * (pairs[at, :, BLOCK:] - row_delta)).astype(BF16)
            acc[j] += jnp.dot(
                jnp.concatenate([weights.astype(BF16), half], axis=1), right[i], preferred_element_type=F32
            )
            halves.append(half)
            keys.append(kt[j])
        return total_qt + jnp.dot(
            jnp.concatenate(keys, axis=1), jnp.concatenate(halves, axis=0), preferred_element_type=F32
        )

    zero = jnp.zeros((8, BLOCK), F32)
    no_grad = jnp.zeros((HEAD_DIM, BLOCK), F32)

    def row_scales(stats):
        total, dotted = stats
        inv_total = 1.0 / jnp.sum(total, axis=0, keepdims=True)
        return inv_total, jnp.sum(dotted, axis=0, keepdims=True) * inv_total

    def rows_in_turn(stats, query_block):
        def two_blocks(step, stats):
            i = first + 2 * step
            stats = query_block(i, i + 1, pairs_even, pairs_odd, stats)
            return query_block(i + 1, jnp.minimum(i + 2, last - 1), pairs_odd, pairs_even, stats)

        lax.fori_loop(0, (last - first) // 2, two_blocks, stats)

    def attend_all():
        def places(i):
            return [(j, j, mask_ref[i * nb + j] > 0) for j in range(nb)]

        def query_block(i, later, mine, other, stats):
            inv_total, row_delta = row_scales(stats)
            grad_qt[i] = grad_group(mine, i, places(i), inv_total, row_delta, no_grad)
            return score_group(other, later, places(later), (zero, zero))

        rows_in_turn(score_group(pairs_even, first, places(first), (zero, zero)), query_block)

    def attend_listed():
        def clear(at, carry):
            pairs_even[at] = jnp.zeros((BLOCK, 2 * BLOCK), F32)
            pairs_odd[at] = jnp.zeros((BLOCK, 2 * BLOCK), F32)
            return carry

        lax.fori_loop(0, slots, clear, 0)

        def groups_of(i):
            return (info_ref[8 + i] + (GROUP - 1)) // GROUP

        def places(i, g):
            spots = [g * GROUP + u for u in range(GROUP)]
            return [(at, list_ref[i * slots + at], at < info_ref[8 + i]) for at in spots]

        def query_block(i, later, mine, other, stats):
            inv_total, row_delta = row_scales(stats)

            def step(g, carry):
                total_qt, total, dotted = carry
                total_qt = grad_group(mine, i, places(i, g), inv_total, row_delta, total_qt)
                return (total_qt, *score_group(other, later, places(later, g), (total, dotted)))

            total_qt, total, dotted = lax.fori_loop(
                0, jnp.maximum(groups_of(i), groups_of(later)), step, (no_grad, zero, zero)
            )
            grad_qt[i] = total_qt
            return total, dotted

        stats = lax.fori_loop(
            0, groups_of(first), lambda g, s: score_group(pairs_even, first, places(first, g), s), (zero, zero)
        )
        rows_in_turn(stats, query_block)

    dense = info_ref[3]
    pl.when(dense > 0)(attend_all)
    pl.when(dense == 0)(attend_listed)

    def finish_queries(step, total):
        for u in range(UNROLL):
            i = first + step * UNROLL + u
            grad, gains = norm_back(in_ref[i, 0].astype(F32), q_gain, grad_qt[i].T * SCALE)
            qk_out[i, 0] = grad.astype(BF16)
            total = total + fold_rows(gains)
        return total

    def finish_keys(step, total):
        for u in range(UNROLL):
            j = step * UNROLL + u
            grad, gains = norm_back(in_ref[j, 1].astype(F32), k_gain, acc[j, :, HEAD_DIM:] * SCALE)
            qk_out[j, 1] = grad.astype(BF16)
            v_out[j] = acc[j, :, :HEAD_DIM].astype(BF16)
            total = total + fold_rows(gains)
        for copy in store(step):
            copy.start()
        return total

    part_ref[0:8, :] = lax.fori_loop(0, (last - first) // UNROLL, finish_queries, zero)
    part_ref[8:16, :] = lax.fori_loop(0, nb // UNROLL, finish_keys, zero)
    for step in range(nb // UNROLL):
        for copy in store(step):
            copy.wait()


def item_grads(info, block_list, mask, gains, arrived):
    nb = arrived.shape[0]
    slots = block_list.shape[0] // nb
    smem = pl.BlockSpec(memory_space=pltpu.SMEM)
    vmem = pl.BlockSpec(memory_space=pltpu.VMEM)
    hbm = pl.BlockSpec(memory_space=pltpu.HBM)
    return pl.pallas_call(
        functools.partial(item_kernel, nb),
        out_shape=(
            jax.ShapeDtypeStruct((nb, 2, BLOCK, HEAD_DIM), BF16),
            jax.ShapeDtypeStruct((nb, BLOCK, HEAD_DIM), BF16),
            jax.ShapeDtypeStruct((16, HEAD_DIM), F32),
        ),
        in_specs=[smem, smem, smem, vmem, hbm],
        out_specs=(hbm, hbm, vmem),
        scratch_shapes=[
            pltpu.VMEM((nb, 4, BLOCK, HEAD_DIM), BF16),
            pltpu.VMEM((nb, 2, BLOCK, HEAD_DIM), BF16),
            pltpu.VMEM((nb, BLOCK, HEAD_DIM), BF16),
            pltpu.SemaphoreType.DMA((nb // UNROLL,)),
            pltpu.SemaphoreType.DMA((nb // UNROLL,)),
            pltpu.SemaphoreType.DMA((nb // UNROLL,)),
            pltpu.VMEM((nb + 1, BLOCK, 2 * HEAD_DIM), BF16),
            pltpu.VMEM((nb + 1, HEAD_DIM, BLOCK), BF16),
            pltpu.VMEM((slots, BLOCK, 2 * BLOCK), F32),
            pltpu.VMEM((slots, BLOCK, 2 * BLOCK), F32),
            pltpu.VMEM((nb + 1, BLOCK, 2 * HEAD_DIM), F32),
            pltpu.VMEM((nb, 2 * HEAD_DIM, 2 * BLOCK), BF16),
            pltpu.VMEM((nb, 2 * BLOCK, 2 * HEAD_DIM), BF16),
            pltpu.VMEM((nb, HEAD_DIM, BLOCK), F32),
            pltpu.VMEM((nb, 8, BLOCK), F32),
        ],
        compiler_params=pltpu.CompilerParams(vmem_limit_bytes=60 * 2**20),
        name="item_grads",
    )(info, block_list, mask, gains, arrived)


def merge_kernel(count, tail_scale, heads_ref, in_ref, *out_refs):
    outs = out_refs[:count]

    def piece(slot, which):
        return in_ref[slot, which * BLOCK : (which + 1) * BLOCK, :]

    def pair(p, carry):
        at = pl.multiple_of(heads_ref[2 * p] * HEAD_DIM, HEAD_DIM)
        for which, out in enumerate(outs):
            both = piece(2 * p, which).astype(F32) + piece(2 * p + 1, which).astype(F32)
            out[:, pl.ds(at, HEAD_DIM)] = both.astype(BF16)
        return carry

    def single(slot, carry):
        at = pl.multiple_of(heads_ref[slot] * HEAD_DIM, HEAD_DIM)
        for which, out in enumerate(outs):
            out[:, pl.ds(at, HEAD_DIM)] = piece(slot, which)
        return carry

    lax.fori_loop(0, SPLITS, pair, 0)
    lax.fori_loop(2 * SPLITS, ITEMS, single, 0)
    if len(out_refs) > count:
        def tail(slot, total):
            return total + in_ref[slot, count * BLOCK : count * BLOCK + 16, :].astype(F32)

        total = lax.fori_loop(0, ITEMS, tail, jnp.zeros((16, HEAD_DIM), F32))
        out_refs[count][...] = (total[0:2] + (total[2:4] + total[4:6])) * tail_scale


def merge(item_heads, returned, count, tail_scale=None):
    vmem = pl.BlockSpec(memory_space=pltpu.VMEM)
    wide = jax.ShapeDtypeStruct((BLOCK, HEADS * HEAD_DIM), BF16)
    shapes = (wide,) * count + ((jax.ShapeDtypeStruct((2, HEAD_DIM), F32),) if tail_scale else ())
    return pl.pallas_call(
        functools.partial(merge_kernel, count, tail_scale),
        out_shape=shapes,
        in_specs=[pl.BlockSpec(memory_space=pltpu.SMEM), vmem],
        out_specs=(vmem,) * len(shapes),
        compiler_params=pltpu.CompilerParams(vmem_limit_bytes=24 * 2**20),
        name="merge_heads",
    )(item_heads, returned)


def attach_kernel(part_ref, v_ref, out_ref):
    total = part_ref[...]
    high = total.astype(BF16)
    rest = total - high.astype(F32)
    middle = rest.astype(BF16)
    low = (rest - middle.astype(F32)).astype(BF16)
    pieces = [high.astype(F32), middle.astype(F32), low.astype(F32), jnp.zeros((10, HEAD_DIM), F32)]
    tail = jnp.concatenate(pieces, axis=0).astype(BF16)

    def move(slot, carry):
        out_ref[slot, :BLOCK, :] = v_ref[slot]
        out_ref[slot, BLOCK:, :] = tail
        return carry

    lax.fori_loop(0, ITEMS, move, 0)


def attach(part, grads_v):
    vmem = pl.BlockSpec(memory_space=pltpu.VMEM)
    return pl.pallas_call(
        attach_kernel,
        out_shape=jax.ShapeDtypeStruct((ITEMS, BLOCK + 16, HEAD_DIM), BF16),
        in_specs=[vmem, vmem],
        out_specs=vmem,
        name="attach_gains",
    )(part, grads_v)


def sum_over_videos(part):
    count = lax.axis_size("dp")
    step = 1
    while step < count:
        part = part + lax.ppermute(part, "dp", [(i, i ^ step) for i in range(count)])
        step *= 2
    return part


def plan_items(block_masks):
    totals = jnp.sum((block_masks > 0).astype(jnp.int32), axis=(1, 2))
    heads = jnp.arange(HEADS, dtype=jnp.int32)
    ahead = (totals[None, :] > totals[:, None]) | (
        (totals[None, :] == totals[:, None]) & (heads[None, :] < heads[:, None])
    )
    rank = jnp.sum(ahead.astype(jnp.int32), axis=1)
    counter = jnp.arange(ITEMS, dtype=jnp.int32)
    wanted = jnp.where(counter < 2 * SPLITS, counter // 2, counter - SPLITS)
    return jnp.sum(jnp.where(rank[None, :] == wanted[:, None], heads[None, :], 0), axis=1)


def block_lists(mask_head):
    nb = mask_head.shape[0]
    on = (mask_head > 0).astype(jnp.int32)
    lower = (jnp.arange(nb)[:, None] < jnp.arange(nb)[None, :]).astype(jnp.int32)
    place = jnp.sum(on[:, :, None] * lower[None, :, :], axis=1)
    slot = jnp.arange(nb, dtype=jnp.int32)
    hit = (on[:, :, None] > 0) & (place[:, :, None] == slot[None, None, :])
    which = jnp.arange(nb, dtype=jnp.int32)[None, :, None]
    counts = jnp.sum(on, axis=1)
    lists = nb + jnp.sum(jnp.where(hit, which - nb, 0), axis=1)
    return counts, lists


def body(q_raw, k_raw, values, grad_out, q_gain, k_gain, block_masks):
    device_rank = lax.axis_index("ulysses")
    tok_rows, width = q_raw.shape[1:]
    nb = block_masks.shape[1]
    seq_len = tok_rows * lax.axis_size("ulysses")
    videos = lax.axis_size("dp")
    item_heads = plan_items(block_masks)
    outgoing = pack(item_heads, q_raw[0], k_raw[0], values[0], grad_out[0])
    arrived = lax.all_to_all(outgoing, "ulysses", split_axis=0, concat_axis=0, tiled=True)
    head = lax.dynamic_index_in_dim(item_heads, device_rank, 0, keepdims=False)
    mask_head = lax.dynamic_index_in_dim(block_masks, head, 0, keepdims=False)
    counts, lists = block_lists(mask_head)
    split = device_rank < 2 * SPLITS
    half = device_rank % 2
    first = jnp.where(split, half * (nb // 2), 0)
    last = jnp.where(split, (half + 1) * (nb // 2), nb)
    bound = 1.02 * HEAD_DIM * SCORE2 * jnp.max(jnp.abs(q_gain)) * jnp.max(jnp.abs(k_gain))
    careful = jnp.where(bound < SAFE_BOUND, 0, 1)
    dense = jnp.where(jnp.max(counts) > DENSE_FROM, 1, 0)
    info = jnp.concatenate(
        [jnp.stack([first, last, careful, dense]).astype(jnp.int32), jnp.zeros((4,), jnp.int32), counts]
    )
    gains = jnp.stack([q_gain, k_gain])
    grads_qk, grads_v, part = item_grads(info, lists.reshape(-1), mask_head.reshape(-1), gains, arrived)
    back_qk = lax.all_to_all(
        grads_qk.reshape(nb, 2 * BLOCK, HEAD_DIM), "ulysses", split_axis=0, concat_axis=0, tiled=True
    )
    part = sum_over_videos(jnp.sum(part.reshape(2, 8, HEAD_DIM), axis=1))
    attached, back_qk = lax.optimization_barrier((attach(part, grads_v), back_qk))
    back_v = lax.all_to_all(attached, "ulysses", split_axis=0, concat_axis=0, tiled=True)
    grad_q, grad_k = merge(item_heads, back_qk, 2)
    grad_v, gain_grads = merge(item_heads, back_v, 1, (videos * seq_len * HEADS) ** (-0.5))
    return (grad_q[None], grad_k[None], grad_v[None], gain_grads)


def solution(mesh):
    tokens = P("dp", "ulysses", None)
    return jax.shard_map(
        body,
        mesh=mesh,
        in_specs=(tokens, tokens, tokens, tokens, P(), P(), P()),
        out_specs=(tokens, tokens, tokens, P()),
        check_vma=False,
    )
```

```python
import functools

import jax
import jax.numpy as jnp
from jax import lax
from jax.experimental import pallas as pl
from jax.experimental.pallas import tpu as pltpu
from jax.sharding import PartitionSpec as P

HEADS = 24
HEAD_DIM = 128
SPLITS = 8
BLOCK = 128
ITEMS = 32
GROUP = 5
DENSE_FROM = 12
CHUNK = 4
UNROLL = 4

NORM_EPS = 1e-06
NEG_FILL = -1e30
SCALE = HEAD_DIM ** (-0.5)
LOG2E = 1.4426950408889634
SCORE2 = SCALE * LOG2E
SAFE_BOUND = 50.0
F32 = jnp.float32
BF16 = jnp.bfloat16


def pack_kernel(heads_ref, q_ref, k_ref, v_ref, o_ref, out_ref, wide, tall, in_sems, out_sems):
    rows = q_ref.shape[0]
    part = rows // CHUNK
    loads, stores = [], []
    for which, src in enumerate((q_ref, k_ref, v_ref, o_ref)):
        for c in range(CHUNK):
            at = pl.ds(c * part, part)
            copy = pltpu.make_async_copy(src.at[at], wide.at[which, at], in_sems.at[which, c])
            copy.start()
            loads.append(copy)
    for which in range(4):
        for c in range(CHUNK):
            loads[which * CHUNK + c].wait()

        def move(slot, carry, which=which):
            at = pl.multiple_of(heads_ref[slot] * HEAD_DIM, HEAD_DIM)
            tall[which, slot] = wide[which, :, pl.ds(at, HEAD_DIM)]
            return carry

        lax.fori_loop(0, ITEMS, move, 0)
        copy = pltpu.make_async_copy(tall.at[which], out_ref.at[:, which], out_sems.at[which])
        copy.start()
        stores.append(copy)
    for copy in stores:
        copy.wait()


def pack(item_heads, q_raw, k_raw, values, grad_out):
    rows, width = q_raw.shape
    hbm = pl.BlockSpec(memory_space=pltpu.HBM)
    return pl.pallas_call(
        pack_kernel,
        out_shape=jax.ShapeDtypeStruct((ITEMS, 4, rows, HEAD_DIM), BF16),
        in_specs=[pl.BlockSpec(memory_space=pltpu.SMEM)] + [hbm] * 4,
        out_specs=hbm,
        scratch_shapes=[
            pltpu.VMEM((4, rows, width), BF16),
            pltpu.VMEM((4, ITEMS, rows, HEAD_DIM), BF16),
            pltpu.SemaphoreType.DMA((4, CHUNK)),
            pltpu.SemaphoreType.DMA((4,)),
        ],
        compiler_params=pltpu.CompilerParams(vmem_limit_bytes=60 * 2**20),
        name="pack_heads",
    )(item_heads, q_raw, k_raw, values, grad_out)


def inv_spread(raw_float):
    return lax.rsqrt(jnp.mean(raw_float * raw_float, axis=-1, keepdims=True) + NORM_EPS)


def norm_back(raw_float, gain, grad_normed):
    inv = inv_spread(raw_float)
    unit = raw_float * inv
    scaled = gain * grad_normed
    inner = jnp.sum(scaled * unit, axis=-1, keepdims=True) * (1.0 / HEAD_DIM)
    return (scaled - unit * inner) * inv, grad_normed * unit


def fold_rows(full):
    return jnp.sum(full.reshape(-1, 8, full.shape[-1]), axis=0)


def item_kernel(
    nb, info_ref, list_ref, mask_ref, gain_ref, hbm_ref, qk_ref, v_ref, part_ref,
    in_ref, qk_out, v_out, in_sems, qk_sems, v_sems, kv, kt, pairs_even, pairs_odd, acc, left, right, grad_qt, shifts,
):
    first, last, careful = info_ref[0], info_ref[1], info_ref[2]
    q_gain = gain_ref[0:1, :]
    k_gain = gain_ref[1:2, :]
    slots = list_ref.shape[0] // nb
    zero_half = jnp.zeros((BLOCK, HEAD_DIM), BF16)

    def load(step):
        at = pl.ds(step * UNROLL, UNROLL)
        return pltpu.make_async_copy(hbm_ref.at[at], in_ref.at[at], in_sems.at[step])

    def store(step):
        at = pl.ds(step * UNROLL, UNROLL)
        return (
            pltpu.make_async_copy(qk_out.at[at], qk_ref.at[at], qk_sems.at[step]),
            pltpu.make_async_copy(v_out.at[at], v_ref.at[at], v_sems.at[step]),
        )

    for step in range(nb // UNROLL):
        load(step).start()

    def prepare_keys(step, carry):
        load(step).wait()
        for u in range(UNROLL):
            j = step * UNROLL + u
            raw = in_ref[j, 1].astype(F32)
            normed = (raw * inv_spread(raw) * k_gain).astype(BF16)
            kv[j, :, :HEAD_DIM] = normed
            kv[j, :, HEAD_DIM:] = in_ref[j, 2]
            kt[j] = normed.T
            acc[j] = jnp.zeros((BLOCK, 2 * HEAD_DIM), F32)
            qk_out[j, 0] = zero_half
            shifts[j] = jnp.zeros((8, BLOCK), F32)
        return carry

    def prepare_query(i, padded):
        raw = in_ref[i, 0].astype(F32)
        normed = (raw * inv_spread(raw) * q_gain).astype(BF16)
        o_block = in_ref[i, 3]
        left[i, :HEAD_DIM, :BLOCK] = normed.T
        left[i, HEAD_DIM:, BLOCK:] = o_block.T
        right[i, :BLOCK, :HEAD_DIM] = o_block
        right[i, BLOCK:, HEAD_DIM:] = normed
        if padded:
            left[i, :HEAD_DIM, BLOCK:] = zero_half
            left[i, HEAD_DIM:, :BLOCK] = zero_half
            right[i, :BLOCK, HEAD_DIM:] = zero_half
            right[i, BLOCK:, :HEAD_DIM] = zero_half

    def prepare_queries(step, carry):
        for u in range(UNROLL):
            prepare_query(first + step * UNROLL + u, True)
        return carry

    def finish_query(i, total_qt):
        grad, gains = norm_back(in_ref[i, 0].astype(F32), q_gain, total_qt.T * SCALE)
        qk_out[i, 0] = grad.astype(BF16)
        return fold_rows(gains)

    lax.fori_loop(0, nb // UNROLL, prepare_keys, 0)
    dense = info_ref[3]
    ahead = jnp.where((dense == 0) | (careful > 0), last - first, 0)
    lax.fori_loop(0, ahead // UNROLL, prepare_queries, 0)
    kv[nb] = jnp.zeros((BLOCK, 2 * HEAD_DIM), BF16)
    kt[nb] = zero_half
    acc[nb] = jnp.zeros((BLOCK, 2 * HEAD_DIM), F32)

    part_ref[...] = jnp.zeros((16, HEAD_DIM), F32)

    @pl.when(careful > 0)
    def _():
        def peak_row(i, carry):
            def peak_step(at, peak):
                j = list_ref[i * slots + at]
                scores = jnp.dot(kv[j, :, :HEAD_DIM], left[i, :HEAD_DIM, :BLOCK], preferred_element_type=F32)
                return jnp.maximum(peak, jnp.max(scores.reshape(-1, 8, BLOCK), axis=0))

            peak = lax.fori_loop(0, info_ref[8 + i], peak_step, jnp.full((8, BLOCK), NEG_FILL, F32))
            shifts[i] = jnp.broadcast_to(jnp.max(peak, axis=0, keepdims=True) * SCORE2, (8, BLOCK))
            return carry

        lax.fori_loop(first, last, peak_row, 0)

    def score_group(pairs, i, places, stats):
        total, dotted = stats
        shift = shifts[i, 0:1, :]
        for at, j, allowed in places:
            both = jnp.dot(kv[j], left[i], preferred_element_type=F32)
            weights = jnp.exp2(both[:, :BLOCK] * SCORE2 + (jnp.where(allowed, 0.0, NEG_FILL) - shift))
            grads = both[:, BLOCK:]
            pairs[at, :, :BLOCK] = weights
            pairs[at, :, BLOCK : 2 * BLOCK] = grads
            total = total + fold_rows(weights)
            dotted = dotted + fold_rows(weights * grads)
        return total, dotted

    def grad_group(pairs, i, places, inv_total, row_delta, total_qt):
        halves, keys = [], []
        for at, j, _ in places:
            weights = pairs[at, :, :BLOCK] * inv_total
            half = (weights * (pairs[at, :, BLOCK : 2 * BLOCK] - row_delta)).astype(BF16)
            acc[j] += jnp.dot(
                jnp.concatenate([weights.astype(BF16), half], axis=1), right[i], preferred_element_type=F32
            )
            halves.append(half)
            keys.append(kt[j])
        return total_qt + jnp.dot(
            jnp.concatenate(keys, axis=1), jnp.concatenate(halves, axis=0), preferred_element_type=F32
        )

    zero = jnp.zeros((8, BLOCK), F32)
    no_grad = jnp.zeros((HEAD_DIM, BLOCK), F32)

    def row_scales(stats):
        total, dotted = stats
        inv_total = 1.0 / jnp.sum(total, axis=0, keepdims=True)
        return inv_total, jnp.sum(dotted, axis=0, keepdims=True) * inv_total

    def in_turn(start, stop, stats, visit):
        def two_visits(step, stats):
            i = start + 2 * step
            stats = visit(i, i + 1, pairs_even, pairs_odd, stats)
            return visit(i + 1, jnp.minimum(i + 2, stop - 1), pairs_odd, pairs_even, stats)

        lax.fori_loop(0, (stop - start) // 2, two_visits, stats)

    def attend_all():
        wide = 2 * BLOCK
        earlier = lax.broadcasted_iota(jnp.int32, (1, wide), 1) < BLOCK
        top, low = slice(0, BLOCK), slice(BLOCK, wide)

        def score_two(pairs, two):
            i = 2 * two
            queries = jnp.concatenate([left[i, top, top], left[i + 1, top, top]], axis=1)
            outs = jnp.concatenate([left[i, low, low], left[i + 1, low, low]], axis=1)
            shift = jnp.concatenate([shifts[i, 0:1, :], shifts[i + 1, 0:1, :]], axis=1)
            total = dotted = jnp.zeros((8, wide), F32)
            for j in range(nb):
                scores = jnp.dot(kv[j, :, :HEAD_DIM], queries, preferred_element_type=F32)
                grads = jnp.dot(kv[j, :, HEAD_DIM:], outs, preferred_element_type=F32)
                bias = jnp.where(
                    earlier,
                    jnp.where(mask_ref[i * nb + j] > 0, 0.0, NEG_FILL),
                    jnp.where(mask_ref[(i + 1) * nb + j] > 0, 0.0, NEG_FILL),
                )
                weights = jnp.exp2(scores * SCORE2 + (bias - shift))
                pairs[j, :, :wide] = weights
                pairs[j, :, wide:] = grads
                total = total + fold_rows(weights)
                dotted = dotted + fold_rows(weights * grads)
            return total, dotted

        def visit(two, later, mine, other, stats):
            i = 2 * two
            for u in range(2):
                prepare_query(2 * later + u, False)
            inv_total, row_delta = row_scales(stats)
            outs = jnp.concatenate([right[i, top, top], right[i + 1, top, top]], axis=0)
            queries = jnp.concatenate([right[i, low, low], right[i + 1, low, low]], axis=0)
            halves = []
            for j in range(nb):
                weights = mine[j, :, :wide] * inv_total
                half = (weights * (mine[j, :, wide:] - row_delta)).astype(BF16)
                acc[j, :, :HEAD_DIM] += jnp.dot(weights.astype(BF16), outs, preferred_element_type=F32)
                acc[j, :, HEAD_DIM:] += jnp.dot(half, queries, preferred_element_type=F32)
                halves.append(half)
            total_qt = jnp.dot(
                jnp.concatenate([kt[j] for j in range(nb)], axis=1),
                jnp.concatenate(halves, axis=0),
                preferred_element_type=F32,
            )
            stats = score_two(other, later)
            part_ref[0:8, :] += finish_query(i, total_qt[:, :BLOCK]) + finish_query(i + 1, total_qt[:, BLOCK:])
            return stats

        for u in range(2):
            prepare_query(first + u, False)
        in_turn(first // 2, last // 2, score_two(pairs_even, first // 2), visit)

    def attend_listed():
        def clear(at, carry):
            pairs_even[at, :, : 2 * BLOCK] = jnp.zeros((BLOCK, 2 * BLOCK), F32)
            pairs_odd[at, :, : 2 * BLOCK] = jnp.zeros((BLOCK, 2 * BLOCK), F32)
            return carry

        lax.fori_loop(0, 2 * GROUP + DENSE_FROM, clear, 0)

        def groups_of(i):
            return (info_ref[8 + i] + (GROUP - 1)) // GROUP

        def places(i, g):
            spots = [g * GROUP + u for u in range(GROUP)]
            return [(at, list_ref[i * slots + at], at < info_ref[8 + i]) for at in spots]

        def query_block(i, later, mine, other, stats):
            inv_total, row_delta = row_scales(stats)

            def step(g, carry):
                total_qt, total, dotted = carry
                total_qt = grad_group(mine, i, places(i, g), inv_total, row_delta, total_qt)
                return (total_qt, *score_group(other, later, places(later, g), (total, dotted)))

            total_qt, total, dotted = lax.fori_loop(
                0, jnp.maximum(groups_of(i), groups_of(later)), step, (no_grad, zero, zero)
            )
            grad_qt[i] = total_qt
            return total, dotted

        stats = lax.fori_loop(
            0, groups_of(first), lambda g, s: score_group(pairs_even, first, places(first, g), s), (zero, zero)
        )
        in_turn(first, last, stats, query_block)

    pl.when(dense > 0)(attend_all)
    pl.when(dense == 0)(attend_listed)

    def finish_queries(step, total):
        for u in range(UNROLL):
            i = first + step * UNROLL + u
            total = total + finish_query(i, grad_qt[i])
        return total

    def finish_keys(step, total):
        for u in range(UNROLL):
            j = step * UNROLL + u
            grad, gains = norm_back(in_ref[j, 1].astype(F32), k_gain, acc[j, :, HEAD_DIM:] * SCALE)
            qk_out[j, 1] = grad.astype(BF16)
            v_out[j] = acc[j, :, :HEAD_DIM].astype(BF16)
            total = total + fold_rows(gains)
        for copy in store(step):
            copy.start()
        return total

    behind = jnp.where(dense == 0, last - first, 0)
    part_ref[0:8, :] += lax.fori_loop(0, behind // UNROLL, finish_queries, zero)
    part_ref[8:16, :] = lax.fori_loop(0, nb // UNROLL, finish_keys, zero)
    for step in range(nb // UNROLL):
        for copy in store(step):
            copy.wait()


def item_grads(info, block_list, mask, gains, arrived):
    nb = arrived.shape[0]
    slots = block_list.shape[0] // nb
    smem = pl.BlockSpec(memory_space=pltpu.SMEM)
    vmem = pl.BlockSpec(memory_space=pltpu.VMEM)
    hbm = pl.BlockSpec(memory_space=pltpu.HBM)
    return pl.pallas_call(
        functools.partial(item_kernel, nb),
        out_shape=(
            jax.ShapeDtypeStruct((nb, 2, BLOCK, HEAD_DIM), BF16),
            jax.ShapeDtypeStruct((nb, BLOCK, HEAD_DIM), BF16),
            jax.ShapeDtypeStruct((16, HEAD_DIM), F32),
        ),
        in_specs=[smem, smem, smem, vmem, hbm],
        out_specs=(hbm, hbm, vmem),
        scratch_shapes=[
            pltpu.VMEM((nb, 4, BLOCK, HEAD_DIM), BF16),
            pltpu.VMEM((nb, 2, BLOCK, HEAD_DIM), BF16),
            pltpu.VMEM((nb, BLOCK, HEAD_DIM), BF16),
            pltpu.SemaphoreType.DMA((nb // UNROLL,)),
            pltpu.SemaphoreType.DMA((nb // UNROLL,)),
            pltpu.SemaphoreType.DMA((nb // UNROLL,)),
            pltpu.VMEM((nb + 1, BLOCK, 2 * HEAD_DIM), BF16),
            pltpu.VMEM((nb + 1, HEAD_DIM, BLOCK), BF16),
            pltpu.VMEM((slots, BLOCK, 4 * BLOCK), F32),
            pltpu.VMEM((slots, BLOCK, 4 * BLOCK), F32),
            pltpu.VMEM((nb + 1, BLOCK, 2 * HEAD_DIM), F32),
            pltpu.VMEM((nb, 2 * HEAD_DIM, 2 * BLOCK), BF16),
            pltpu.VMEM((nb, 2 * BLOCK, 2 * HEAD_DIM), BF16),
            pltpu.VMEM((nb, HEAD_DIM, BLOCK), F32),
            pltpu.VMEM((nb, 8, BLOCK), F32),
        ],
        compiler_params=pltpu.CompilerParams(vmem_limit_bytes=60 * 2**20),
        name="item_grads",
    )(info, block_list, mask, gains, arrived)


def merge_kernel(count, tail_scale, heads_ref, in_ref, *out_refs):
    outs = out_refs[:count]

    def piece(slot, which):
        return in_ref[slot, which * BLOCK : (which + 1) * BLOCK, :]

    def pair(p, carry):
        at = pl.multiple_of(heads_ref[2 * p] * HEAD_DIM, HEAD_DIM)
        for which, out in enumerate(outs):
            both = piece(2 * p, which).astype(F32) + piece(2 * p + 1, which).astype(F32)
            out[:, pl.ds(at, HEAD_DIM)] = both.astype(BF16)
        return carry

    def single(slot, carry):
        at = pl.multiple_of(heads_ref[slot] * HEAD_DIM, HEAD_DIM)
        for which, out in enumerate(outs):
            out[:, pl.ds(at, HEAD_DIM)] = piece(slot, which)
        return carry

    lax.fori_loop(0, SPLITS, pair, 0)
    lax.fori_loop(2 * SPLITS, ITEMS, single, 0)
    if len(out_refs) > count:
        def tail(slot, total):
            return total + in_ref[slot, count * BLOCK : count * BLOCK + 16, :].astype(F32)

        total = lax.fori_loop(0, ITEMS, tail, jnp.zeros((16, HEAD_DIM), F32))
        out_refs[count][...] = (total[0:2] + (total[2:4] + total[4:6])) * tail_scale


def merge(item_heads, returned, count, tail_scale=None):
    vmem = pl.BlockSpec(memory_space=pltpu.VMEM)
    wide = jax.ShapeDtypeStruct((BLOCK, HEADS * HEAD_DIM), BF16)
    shapes = (wide,) * count + ((jax.ShapeDtypeStruct((2, HEAD_DIM), F32),) if tail_scale else ())
    return pl.pallas_call(
        functools.partial(merge_kernel, count, tail_scale),
        out_shape=shapes,
        in_specs=[pl.BlockSpec(memory_space=pltpu.SMEM), vmem],
        out_specs=(vmem,) * len(shapes),
        compiler_params=pltpu.CompilerParams(vmem_limit_bytes=24 * 2**20),
        name="merge_heads",
    )(item_heads, returned)


def attach_kernel(part_ref, v_ref, out_ref):
    total = part_ref[...]
    high = total.astype(BF16)
    rest = total - high.astype(F32)
    middle = rest.astype(BF16)
    low = (rest - middle.astype(F32)).astype(BF16)
    pieces = [high.astype(F32), middle.astype(F32), low.astype(F32), jnp.zeros((10, HEAD_DIM), F32)]
    tail = jnp.concatenate(pieces, axis=0).astype(BF16)

    def move(slot, carry):
        out_ref[slot, :BLOCK, :] = v_ref[slot]
        out_ref[slot, BLOCK:, :] = tail
        return carry

    lax.fori_loop(0, ITEMS, move, 0)


def attach(part, grads_v):
    vmem = pl.BlockSpec(memory_space=pltpu.VMEM)
    return pl.pallas_call(
        attach_kernel,
        out_shape=jax.ShapeDtypeStruct((ITEMS, BLOCK + 16, HEAD_DIM), BF16),
        in_specs=[vmem, vmem],
        out_specs=vmem,
        name="attach_gains",
    )(part, grads_v)


def sum_over_videos(part):
    count = lax.axis_size("dp")
    step = 1
    while step < count:
        part = part + lax.ppermute(part, "dp", [(i, i ^ step) for i in range(count)])
        step *= 2
    return part


def plan_items(block_masks):
    totals = jnp.sum((block_masks > 0).astype(jnp.int32), axis=(1, 2))
    heads = jnp.arange(HEADS, dtype=jnp.int32)
    ahead = (totals[None, :] > totals[:, None]) | (
        (totals[None, :] == totals[:, None]) & (heads[None, :] < heads[:, None])
    )
    rank = jnp.sum(ahead.astype(jnp.int32), axis=1)
    counter = jnp.arange(ITEMS, dtype=jnp.int32)
    wanted = jnp.where(counter < 2 * SPLITS, counter // 2, counter - SPLITS)
    return jnp.sum(jnp.where(rank[None, :] == wanted[:, None], heads[None, :], 0), axis=1)


def block_lists(mask_head):
    nb = mask_head.shape[0]
    on = (mask_head > 0).astype(jnp.int32)
    lower = (jnp.arange(nb)[:, None] < jnp.arange(nb)[None, :]).astype(jnp.int32)
    place = jnp.sum(on[:, :, None] * lower[None, :, :], axis=1)
    slot = jnp.arange(nb, dtype=jnp.int32)
    hit = (on[:, :, None] > 0) & (place[:, :, None] == slot[None, None, :])
    which = jnp.arange(nb, dtype=jnp.int32)[None, :, None]
    counts = jnp.sum(on, axis=1)
    lists = nb + jnp.sum(jnp.where(hit, which - nb, 0), axis=1)
    return counts, lists


def body(q_raw, k_raw, values, grad_out, q_gain, k_gain, block_masks):
    device_rank = lax.axis_index("ulysses")
    tok_rows, width = q_raw.shape[1:]
    nb = block_masks.shape[1]
    seq_len = tok_rows * lax.axis_size("ulysses")
    videos = lax.axis_size("dp")
    item_heads = plan_items(block_masks)
    outgoing = pack(item_heads, q_raw[0], k_raw[0], values[0], grad_out[0])
    arrived = lax.all_to_all(outgoing, "ulysses", split_axis=0, concat_axis=0, tiled=True)
    head = lax.dynamic_index_in_dim(item_heads, device_rank, 0, keepdims=False)
    mask_head = lax.dynamic_index_in_dim(block_masks, head, 0, keepdims=False)
    counts, lists = block_lists(mask_head)
    split = device_rank < 2 * SPLITS
    half = device_rank % 2
    first = jnp.where(split, half * (nb // 2), 0)
    last = jnp.where(split, (half + 1) * (nb // 2), nb)
    bound = 1.02 * HEAD_DIM * SCORE2 * jnp.max(jnp.abs(q_gain)) * jnp.max(jnp.abs(k_gain))
    careful = jnp.where(bound < SAFE_BOUND, 0, 1)
    dense = jnp.where(jnp.max(counts) > DENSE_FROM, 1, 0)
    info = jnp.concatenate(
        [jnp.stack([first, last, careful, dense]).astype(jnp.int32), jnp.zeros((4,), jnp.int32), counts]
    )
    gains = jnp.stack([q_gain, k_gain])
    grads_qk, grads_v, part = item_grads(info, lists.reshape(-1), mask_head.reshape(-1), gains, arrived)
    back_qk = lax.all_to_all(
        grads_qk.reshape(nb, 2 * BLOCK, HEAD_DIM), "ulysses", split_axis=0, concat_axis=0, tiled=True
    )
    part = sum_over_videos(jnp.sum(part.reshape(2, 8, HEAD_DIM), axis=1))
    attached, back_qk = lax.optimization_barrier((attach(part, grads_v), back_qk))
    back_v = lax.all_to_all(attached, "ulysses", split_axis=0, concat_axis=0, tiled=True)
    grad_q, grad_k = merge(item_heads, back_qk, 2)
    grad_v, gain_grads = merge(item_heads, back_v, 1, (videos * seq_len * HEADS) ** (-0.5))
    return (grad_q[None], grad_k[None], grad_v[None], gain_grads)


def solution(mesh):
    tokens = P("dp", "ulysses", None)
    return jax.shard_map(
        body,
        mesh=mesh,
        in_specs=(tokens, tokens, tokens, tokens, P(), P(), P()),
        out_specs=(tokens, tokens, tokens, P()),
        check_vma=False,
    )
```

```python
import functools

import jax
import jax.numpy as jnp
from jax import lax
from jax.experimental import pallas as pl
from jax.experimental.pallas import tpu as pltpu
from jax.sharding import PartitionSpec as P

HEADS = 24
HEAD_DIM = 128
SPLITS = 8
BLOCK = 128
ITEMS = 32
GROUP = 5
DENSE_FROM = 12
CHUNK = 4
UNROLL = 4

NORM_EPS = 1e-06
NEG_FILL = -1e30
SCALE = HEAD_DIM ** (-0.5)
LOG2E = 1.4426950408889634
SCORE2 = SCALE * LOG2E
SAFE_BOUND = 50.0
F32 = jnp.float32
BF16 = jnp.bfloat16


def plan_items(mask):
    on = jnp.where(mask > 0, 1.0, 0.0)
    totals = jnp.sum(jnp.sum(on, axis=1), axis=1, keepdims=True)
    shape = (HEADS, HEAD_DIM)
    head = lax.broadcasted_iota(jnp.int32, shape, 0)
    lane = lax.broadcasted_iota(jnp.int32, shape, 1)
    across = jnp.sum(jnp.where(head == lane, totals, 0.0), axis=0, keepdims=True)
    ahead = (across > totals) | ((across == totals) & (lane < head))
    rank = jnp.sum(jnp.where(ahead & (lane < HEADS), 1.0, 0.0), axis=1, keepdims=True)
    wanted = jnp.where(lane < 2 * SPLITS, lane >> 1, lane - SPLITS).astype(F32)
    return jnp.sum(jnp.where(rank == wanted, head.astype(F32), 0.0), axis=0, keepdims=True).astype(jnp.int32)


def pack_kernel(
    mask_ref, q_ref, k_ref, v_ref, o_ref, out_ref, plan_ref,
    wide, tall, heads_ref, in_sems, out_sems, plan_sem,
):
    rows = q_ref.shape[0]
    part = rows // CHUNK
    loads, stores = [], []
    for which, src in enumerate((q_ref, k_ref, v_ref, o_ref)):
        for c in range(CHUNK):
            at = pl.ds(c * part, part)
            copy = pltpu.make_async_copy(src.at[at], wide.at[which, at], in_sems.at[which, c])
            copy.start()
            loads.append(copy)
    plan_ref[...] = jnp.broadcast_to(plan_items(mask_ref[...]), plan_ref.shape)
    copy = pltpu.make_async_copy(plan_ref, heads_ref, plan_sem)
    copy.start()
    copy.wait()
    for which in range(4):
        for c in range(CHUNK):
            loads[which * CHUNK + c].wait()

        def move(slot, carry, which=which):
            at = pl.multiple_of(heads_ref[0, slot] * HEAD_DIM, HEAD_DIM)
            tall[which, slot] = wide[which, :, pl.ds(at, HEAD_DIM)]
            return carry

        lax.fori_loop(0, ITEMS, move, 0)
        copy = pltpu.make_async_copy(tall.at[which], out_ref.at[:, which], out_sems.at[which])
        copy.start()
        stores.append(copy)
    for copy in stores:
        copy.wait()


def pack(block_masks, q_raw, k_raw, values, grad_out):
    rows, width = q_raw.shape
    vmem = pl.BlockSpec(memory_space=pltpu.VMEM)
    hbm = pl.BlockSpec(memory_space=pltpu.HBM)
    return pl.pallas_call(
        pack_kernel,
        out_shape=(
            jax.ShapeDtypeStruct((ITEMS, 4, rows, HEAD_DIM), BF16),
            jax.ShapeDtypeStruct((8, HEAD_DIM), jnp.int32),
        ),
        in_specs=[vmem] + [hbm] * 4,
        out_specs=(hbm, vmem),
        scratch_shapes=[
            pltpu.VMEM((4, rows, width), BF16),
            pltpu.VMEM((4, ITEMS, rows, HEAD_DIM), BF16),
            pltpu.SMEM((8, HEAD_DIM), jnp.int32),
            pltpu.SemaphoreType.DMA((4, CHUNK)),
            pltpu.SemaphoreType.DMA((4,)),
            pltpu.SemaphoreType.DMA,
        ],
        compiler_params=pltpu.CompilerParams(vmem_limit_bytes=60 * 2**20),
        name="pack_heads",
    )(block_masks, q_raw, k_raw, values, grad_out)


def inv_spread(raw_float):
    return lax.rsqrt(jnp.mean(raw_float * raw_float, axis=-1, keepdims=True) + NORM_EPS)


def norm_back(raw_float, gain, grad_normed):
    inv = inv_spread(raw_float)
    unit = raw_float * inv
    scaled = gain * grad_normed
    inner = jnp.sum(scaled * unit, axis=-1, keepdims=True) * (1.0 / HEAD_DIM)
    return (scaled - unit * inner) * inv, grad_normed * unit


def fold_rows(full):
    return jnp.sum(full.reshape(-1, 8, full.shape[-1]), axis=0)


def item_kernel(
    nb, info_ref, list_ref, mask_ref, gain_ref, hbm_ref, qk_ref, v_ref, part_ref,
    in_ref, qk_out, v_out, in_sems, qk_sems, v_sems, kv, kt, pairs_even, pairs_odd, acc, left, right, grad_qt, shifts,
):
    first, last, careful = info_ref[0], info_ref[1], info_ref[2]
    q_gain = gain_ref[0:1, :]
    k_gain = gain_ref[1:2, :]
    slots = list_ref.shape[0] // nb
    zero_half = jnp.zeros((BLOCK, HEAD_DIM), BF16)

    def load(step):
        at = pl.ds(step * UNROLL, UNROLL)
        return pltpu.make_async_copy(hbm_ref.at[at], in_ref.at[at], in_sems.at[step])

    def store(step):
        at = pl.ds(step * UNROLL, UNROLL)
        return (
            pltpu.make_async_copy(qk_out.at[at], qk_ref.at[at], qk_sems.at[step]),
            pltpu.make_async_copy(v_out.at[at], v_ref.at[at], v_sems.at[step]),
        )

    for step in range(nb // UNROLL):
        load(step).start()

    def prepare_keys(step, carry):
        load(step).wait()
        for u in range(UNROLL):
            j = step * UNROLL + u
            raw = in_ref[j, 1].astype(F32)
            normed = (raw * inv_spread(raw) * k_gain).astype(BF16)
            kv[j, :, :HEAD_DIM] = normed
            kv[j, :, HEAD_DIM:] = in_ref[j, 2]
            kt[j] = normed.T
            acc[j] = jnp.zeros((BLOCK, 2 * HEAD_DIM), F32)
            qk_out[j, 0] = zero_half
            shifts[j] = jnp.zeros((8, BLOCK), F32)
        return carry

    def prepare_query(i, padded):
        raw = in_ref[i, 0].astype(F32)
        normed = (raw * inv_spread(raw) * q_gain).astype(BF16)
        o_block = in_ref[i, 3]
        left[i, :HEAD_DIM, :BLOCK] = normed.T
        left[i, HEAD_DIM:, BLOCK:] = o_block.T
        right[i, :BLOCK, :HEAD_DIM] = o_block
        right[i, BLOCK:, HEAD_DIM:] = normed
        if padded:
            left[i, :HEAD_DIM, BLOCK:] = zero_half
            left[i, HEAD_DIM:, :BLOCK] = zero_half
            right[i, :BLOCK, HEAD_DIM:] = zero_half
            right[i, BLOCK:, :HEAD_DIM] = zero_half

    def prepare_queries(step, carry):
        for u in range(UNROLL):
            prepare_query(first + step * UNROLL + u, True)
        return carry

    def finish_key(j):
        grad, gains = norm_back(in_ref[j, 1].astype(F32), k_gain, acc[j, :, HEAD_DIM:] * SCALE)
        qk_out[j, 1] = grad.astype(BF16)
        v_out[j] = acc[j, :, :HEAD_DIM].astype(BF16)
        return fold_rows(gains)

    def finish_keys(step, total):
        for u in range(UNROLL):
            total = total + finish_key(step * UNROLL + u)
        for copy in store(step):
            copy.start()
        return total

    def finish_query(i, total_qt):
        grad, gains = norm_back(in_ref[i, 0].astype(F32), q_gain, total_qt.T * SCALE)
        qk_out[i, 0] = grad.astype(BF16)
        return fold_rows(gains)

    lax.fori_loop(0, nb // UNROLL, prepare_keys, 0)
    dense = info_ref[3]
    ahead = jnp.where((dense == 0) | (careful > 0), last - first, 0)
    lax.fori_loop(0, ahead // UNROLL, prepare_queries, 0)
    kv[nb] = jnp.zeros((BLOCK, 2 * HEAD_DIM), BF16)
    kt[nb] = zero_half
    acc[nb] = jnp.zeros((BLOCK, 2 * HEAD_DIM), F32)

    part_ref[...] = jnp.zeros((16, HEAD_DIM), F32)

    @pl.when(careful > 0)
    def _():
        def peak_row(i, carry):
            def peak_step(at, peak):
                j = list_ref[i * slots + at]
                scores = jnp.dot(kv[j, :, :HEAD_DIM], left[i, :HEAD_DIM, :BLOCK], preferred_element_type=F32)
                return jnp.maximum(peak, jnp.max(scores.reshape(-1, 8, BLOCK), axis=0))

            peak = lax.fori_loop(0, info_ref[8 + i], peak_step, jnp.full((8, BLOCK), NEG_FILL, F32))
            shifts[i] = jnp.broadcast_to(jnp.max(peak, axis=0, keepdims=True) * SCORE2, (8, BLOCK))
            return carry

        lax.fori_loop(first, last, peak_row, 0)

    def score_group(pairs, i, places, stats):
        total, dotted = stats
        shift = shifts[i, 0:1, :]
        for at, j, allowed in places:
            both = jnp.dot(kv[j], left[i], preferred_element_type=F32)
            weights = jnp.exp2(both[:, :BLOCK] * SCORE2 + (jnp.where(allowed, 0.0, NEG_FILL) - shift))
            grads = both[:, BLOCK:]
            pairs[at, :, :BLOCK] = weights
            pairs[at, :, BLOCK : 2 * BLOCK] = grads
            total = total + fold_rows(weights)
            dotted = dotted + fold_rows(weights * grads)
        return total, dotted

    def grad_group(pairs, i, places, inv_total, row_delta, total_qt):
        halves, keys = [], []
        for at, j, _ in places:
            weights = pairs[at, :, :BLOCK] * inv_total
            half = (weights * (pairs[at, :, BLOCK : 2 * BLOCK] - row_delta)).astype(BF16)
            acc[j] += jnp.dot(
                jnp.concatenate([weights.astype(BF16), half], axis=1), right[i], preferred_element_type=F32
            )
            halves.append(half)
            keys.append(kt[j])
        return total_qt + jnp.dot(
            jnp.concatenate(keys, axis=1), jnp.concatenate(halves, axis=0), preferred_element_type=F32
        )

    zero = jnp.zeros((8, BLOCK), F32)
    no_grad = jnp.zeros((HEAD_DIM, BLOCK), F32)

    def row_scales(stats):
        total, dotted = stats
        inv_total = 1.0 / jnp.sum(total, axis=0, keepdims=True)
        return inv_total, jnp.sum(dotted, axis=0, keepdims=True) * inv_total

    def in_turn(start, stop, stats, visit):
        def two_visits(step, stats):
            i = start + 2 * step
            stats = visit(i, i + 1, pairs_even, pairs_odd, stats)
            return visit(i + 1, jnp.minimum(i + 2, stop - 1), pairs_odd, pairs_even, stats)

        lax.fori_loop(0, (stop - start) // 2, two_visits, stats)

    def attend_all():
        wide = 2 * BLOCK
        earlier = lax.broadcasted_iota(jnp.int32, (1, wide), 1) < BLOCK
        top, low = slice(0, BLOCK), slice(BLOCK, wide)

        def score_two(pairs, two):
            i = 2 * two
            queries = jnp.concatenate([left[i, top, top], left[i + 1, top, top]], axis=1)
            outs = jnp.concatenate([left[i, low, low], left[i + 1, low, low]], axis=1)
            shift = jnp.concatenate([shifts[i, 0:1, :], shifts[i + 1, 0:1, :]], axis=1)
            total = dotted = jnp.zeros((8, wide), F32)
            for j in range(nb):
                scores = jnp.dot(kv[j, :, :HEAD_DIM], queries, preferred_element_type=F32)
                grads = jnp.dot(kv[j, :, HEAD_DIM:], outs, preferred_element_type=F32)
                bias = jnp.where(
                    earlier,
                    jnp.where(mask_ref[i * nb + j] > 0, 0.0, NEG_FILL),
                    jnp.where(mask_ref[(i + 1) * nb + j] > 0, 0.0, NEG_FILL),
                )
                weights = jnp.exp2(scores * SCORE2 + (bias - shift))
                pairs[j, :, :wide] = weights
                pairs[j, :, wide:] = grads
                total = total + fold_rows(weights)
                dotted = dotted + fold_rows(weights * grads)
            return total, dotted

        def grads_of_two(mine, two, stats):
            i = 2 * two
            inv_total, row_delta = row_scales(stats)
            outs = jnp.concatenate([right[i, top, top], right[i + 1, top, top]], axis=0)
            queries = jnp.concatenate([right[i, low, low], right[i + 1, low, low]], axis=0)
            halves = []
            for j in range(nb):
                weights = mine[j, :, :wide] * inv_total
                half = (weights * (mine[j, :, wide:] - row_delta)).astype(BF16)
                acc[j, :, :HEAD_DIM] += jnp.dot(weights.astype(BF16), outs, preferred_element_type=F32)
                acc[j, :, HEAD_DIM:] += jnp.dot(half, queries, preferred_element_type=F32)
                halves.append(half)
            return jnp.dot(
                jnp.concatenate([kt[j] for j in range(nb)], axis=1),
                jnp.concatenate(halves, axis=0),
                preferred_element_type=F32,
            )

        def finish_two(two, total_qt):
            part_ref[0:8, :] += finish_query(2 * two, total_qt[:, :BLOCK]) + finish_query(
                2 * two + 1, total_qt[:, BLOCK:]
            )

        def visit(two, mine, other, stats):
            for u in range(2):
                prepare_query(2 * two + 2 + u, False)
            total_qt = grads_of_two(mine, two, stats)
            stats = score_two(other, two + 1)
            finish_two(two, total_qt)
            return stats

        for u in range(2):
            prepare_query(first + u, False)
        start, stop = first // 2, last // 2

        def two_visits(step, stats):
            stats = visit(start + 2 * step, pairs_even, pairs_odd, stats)
            return visit(start + 2 * step + 1, pairs_odd, pairs_even, stats)

        stats = lax.fori_loop(0, (stop - start) // 2 - 1, two_visits, score_two(pairs_even, start))
        stats = visit(stop - 2, pairs_even, pairs_odd, stats)
        finish_two(stop - 1, grads_of_two(pairs_odd, stop - 1, stats))
        total = zero
        for step in range(nb // UNROLL):
            total = finish_keys(step, total)
        part_ref[8:16, :] += total

    def attend_listed():
        def clear(at, carry):
            pairs_even[at, :, : 2 * BLOCK] = jnp.zeros((BLOCK, 2 * BLOCK), F32)
            pairs_odd[at, :, : 2 * BLOCK] = jnp.zeros((BLOCK, 2 * BLOCK), F32)
            return carry

        lax.fori_loop(0, 2 * GROUP + DENSE_FROM, clear, 0)

        def groups_of(i):
            return (info_ref[8 + i] + (GROUP - 1)) // GROUP

        def places(i, g):
            spots = [g * GROUP + u for u in range(GROUP)]
            return [(at, list_ref[i * slots + at], at < info_ref[8 + i]) for at in spots]

        def query_block(i, later, mine, other, stats):
            inv_total, row_delta = row_scales(stats)

            def step(g, carry):
                total_qt, total, dotted = carry
                total_qt = grad_group(mine, i, places(i, g), inv_total, row_delta, total_qt)
                return (total_qt, *score_group(other, later, places(later, g), (total, dotted)))

            total_qt, total, dotted = lax.fori_loop(
                0, jnp.maximum(groups_of(i), groups_of(later)), step, (no_grad, zero, zero)
            )
            grad_qt[i] = total_qt
            return total, dotted

        stats = lax.fori_loop(
            0, groups_of(first), lambda g, s: score_group(pairs_even, first, places(first, g), s), (zero, zero)
        )
        in_turn(first, last, stats, query_block)

    pl.when(dense > 0)(attend_all)
    pl.when(dense == 0)(attend_listed)

    def finish_queries(step, total):
        for u in range(UNROLL):
            i = first + step * UNROLL + u
            total = total + finish_query(i, grad_qt[i])
        return total

    behind = jnp.where(dense == 0, last - first, 0)
    part_ref[0:8, :] += lax.fori_loop(0, behind // UNROLL, finish_queries, zero)
    part_ref[8:16, :] += lax.fori_loop(0, jnp.where(dense == 0, nb // UNROLL, 0), finish_keys, zero)
    for step in range(nb // UNROLL):
        for copy in store(step):
            copy.wait()


def item_grads(info, block_list, mask, gains, arrived):
    nb = arrived.shape[0]
    slots = block_list.shape[0] // nb
    smem = pl.BlockSpec(memory_space=pltpu.SMEM)
    vmem = pl.BlockSpec(memory_space=pltpu.VMEM)
    hbm = pl.BlockSpec(memory_space=pltpu.HBM)
    return pl.pallas_call(
        functools.partial(item_kernel, nb),
        out_shape=(
            jax.ShapeDtypeStruct((nb, 2, BLOCK, HEAD_DIM), BF16),
            jax.ShapeDtypeStruct((nb, BLOCK, HEAD_DIM), BF16),
            jax.ShapeDtypeStruct((16, HEAD_DIM), F32),
        ),
        in_specs=[smem, smem, smem, vmem, hbm],
        out_specs=(hbm, hbm, vmem),
        scratch_shapes=[
            pltpu.VMEM((nb, 4, BLOCK, HEAD_DIM), BF16),
            pltpu.VMEM((nb, 2, BLOCK, HEAD_DIM), BF16),
            pltpu.VMEM((nb, BLOCK, HEAD_DIM), BF16),
            pltpu.SemaphoreType.DMA((nb // UNROLL,)),
            pltpu.SemaphoreType.DMA((nb // UNROLL,)),
            pltpu.SemaphoreType.DMA((nb // UNROLL,)),
            pltpu.VMEM((nb + 1, BLOCK, 2 * HEAD_DIM), BF16),
            pltpu.VMEM((nb + 1, HEAD_DIM, BLOCK), BF16),
            pltpu.VMEM((slots, BLOCK, 4 * BLOCK), F32),
            pltpu.VMEM((slots, BLOCK, 4 * BLOCK), F32),
            pltpu.VMEM((nb + 1, BLOCK, 2 * HEAD_DIM), F32),
            pltpu.VMEM((nb, 2 * HEAD_DIM, 2 * BLOCK), BF16),
            pltpu.VMEM((nb, 2 * BLOCK, 2 * HEAD_DIM), BF16),
            pltpu.VMEM((nb, HEAD_DIM, BLOCK), F32),
            pltpu.VMEM((nb, 8, BLOCK), F32),
        ],
        compiler_params=pltpu.CompilerParams(vmem_limit_bytes=60 * 2**20),
        name="item_grads",
    )(info, block_list, mask, gains, arrived)


def merge_kernel(count, tail_scale, heads_ref, in_ref, *out_refs):
    outs = out_refs[:count]

    def piece(slot, which):
        return in_ref[slot, which * BLOCK : (which + 1) * BLOCK, :]

    def pair(p, carry):
        at = pl.multiple_of(heads_ref[2 * p] * HEAD_DIM, HEAD_DIM)
        for which, out in enumerate(outs):
            both = piece(2 * p, which).astype(F32) + piece(2 * p + 1, which).astype(F32)
            out[:, pl.ds(at, HEAD_DIM)] = both.astype(BF16)
        return carry

    def single(slot, carry):
        at = pl.multiple_of(heads_ref[slot] * HEAD_DIM, HEAD_DIM)
        for which, out in enumerate(outs):
            out[:, pl.ds(at, HEAD_DIM)] = piece(slot, which)
        return carry

    lax.fori_loop(0, SPLITS, pair, 0)
    lax.fori_loop(2 * SPLITS, ITEMS, single, 0)
    if len(out_refs) > count:
        def tail(slot, total):
            return total + in_ref[slot, count * BLOCK : count * BLOCK + 16, :].astype(F32)

        total = lax.fori_loop(0, ITEMS, tail, jnp.zeros((16, HEAD_DIM), F32))
        out_refs[count][...] = (total[0:2] + (total[2:4] + total[4:6])) * tail_scale


def merge(item_heads, returned, count, tail_scale=None):
    vmem = pl.BlockSpec(memory_space=pltpu.VMEM)
    wide = jax.ShapeDtypeStruct((BLOCK, HEADS * HEAD_DIM), BF16)
    shapes = (wide,) * count + ((jax.ShapeDtypeStruct((2, HEAD_DIM), F32),) if tail_scale else ())
    return pl.pallas_call(
        functools.partial(merge_kernel, count, tail_scale),
        out_shape=shapes,
        in_specs=[pl.BlockSpec(memory_space=pltpu.SMEM), vmem],
        out_specs=(vmem,) * len(shapes),
        compiler_params=pltpu.CompilerParams(vmem_limit_bytes=24 * 2**20),
        name="merge_heads",
    )(item_heads, returned)


def attach_kernel(part_ref, v_ref, out_ref):
    total = part_ref[...]
    high = total.astype(BF16)
    rest = total - high.astype(F32)
    middle = rest.astype(BF16)
    low = (rest - middle.astype(F32)).astype(BF16)
    pieces = [high.astype(F32), middle.astype(F32), low.astype(F32), jnp.zeros((10, HEAD_DIM), F32)]
    tail = jnp.concatenate(pieces, axis=0).astype(BF16)

    def move(slot, carry):
        out_ref[slot, :BLOCK, :] = v_ref[slot]
        out_ref[slot, BLOCK:, :] = tail
        return carry

    lax.fori_loop(0, ITEMS, move, 0)


def attach(part, grads_v):
    vmem = pl.BlockSpec(memory_space=pltpu.VMEM)
    return pl.pallas_call(
        attach_kernel,
        out_shape=jax.ShapeDtypeStruct((ITEMS, BLOCK + 16, HEAD_DIM), BF16),
        in_specs=[vmem, vmem],
        out_specs=vmem,
        name="attach_gains",
    )(part, grads_v)


def sum_over_videos(part):
    count = lax.axis_size("dp")
    step = 1
    while step < count:
        part = part + lax.ppermute(part, "dp", [(i, i ^ step) for i in range(count)])
        step *= 2
    return part


def block_lists(mask_head):
    nb = mask_head.shape[0]
    on = (mask_head > 0).astype(jnp.int32)
    lower = (jnp.arange(nb)[:, None] < jnp.arange(nb)[None, :]).astype(jnp.int32)
    place = jnp.sum(on[:, :, None] * lower[None, :, :], axis=1)
    slot = jnp.arange(nb, dtype=jnp.int32)
    hit = (on[:, :, None] > 0) & (place[:, :, None] == slot[None, None, :])
    which = jnp.arange(nb, dtype=jnp.int32)[None, :, None]
    counts = jnp.sum(on, axis=1)
    lists = nb + jnp.sum(jnp.where(hit, which - nb, 0), axis=1)
    return counts, lists


def body(q_raw, k_raw, values, grad_out, q_gain, k_gain, block_masks):
    device_rank = lax.axis_index("ulysses")
    tok_rows, width = q_raw.shape[1:]
    nb = block_masks.shape[1]
    seq_len = tok_rows * lax.axis_size("ulysses")
    videos = lax.axis_size("dp")
    outgoing, plan = pack(block_masks, q_raw[0], k_raw[0], values[0], grad_out[0])
    item_heads = plan[0, :ITEMS]
    arrived = lax.all_to_all(outgoing, "ulysses", split_axis=0, concat_axis=0, tiled=True)
    head = lax.dynamic_index_in_dim(item_heads, device_rank, 0, keepdims=False)
    mask_head = lax.dynamic_index_in_dim(block_masks, head, 0, keepdims=False)
    counts, lists = block_lists(mask_head)
    split = device_rank < 2 * SPLITS
    half = device_rank % 2
    first = jnp.where(split, half * (nb // 2), 0)
    last = jnp.where(split, (half + 1) * (nb // 2), nb)
    bound = 1.02 * HEAD_DIM * SCORE2 * jnp.max(jnp.abs(q_gain)) * jnp.max(jnp.abs(k_gain))
    careful = jnp.where(bound < SAFE_BOUND, 0, 1)
    dense = jnp.where(jnp.max(counts) > DENSE_FROM, 1, 0)
    info = jnp.concatenate(
        [jnp.stack([first, last, careful, dense]).astype(jnp.int32), jnp.zeros((4,), jnp.int32), counts]
    )
    gains = jnp.stack([q_gain, k_gain])
    grads_qk, grads_v, part = item_grads(info, lists.reshape(-1), mask_head.reshape(-1), gains, arrived)
    back_qk = lax.all_to_all(
        grads_qk.reshape(nb, 2 * BLOCK, HEAD_DIM), "ulysses", split_axis=0, concat_axis=0, tiled=True
    )
    part = sum_over_videos(jnp.sum(part.reshape(2, 8, HEAD_DIM), axis=1))
    attached, back_qk = lax.optimization_barrier((attach(part, grads_v), back_qk))
    back_v = lax.all_to_all(attached, "ulysses", split_axis=0, concat_axis=0, tiled=True)
    grad_q, grad_k = merge(item_heads, back_qk, 2)
    grad_v, gain_grads = merge(item_heads, back_v, 1, (videos * seq_len * HEADS) ** (-0.5))
    return (grad_q[None], grad_k[None], grad_v[None], gain_grads)


def solution(mesh):
    tokens = P("dp", "ulysses", None)
    return jax.shard_map(
        body,
        mesh=mesh,
        in_specs=(tokens, tokens, tokens, tokens, P(), P(), P()),
        out_specs=(tokens, tokens, tokens, P()),
        check_vma=False,
    )
```

```python
import functools

import jax
import jax.numpy as jnp
from jax import lax
from jax.experimental import pallas as pl
from jax.experimental.pallas import tpu as pltpu
from jax.sharding import PartitionSpec as P

HEADS = 24
HEAD_DIM = 128
SPLITS = 8
BLOCK = 128
ITEMS = 32
GROUP = 5
DENSE_FROM = 12
CHUNK = 1
UNROLL = 8

NORM_EPS = 1e-06
NEG_FILL = -1e30
SCALE = HEAD_DIM ** (-0.5)
LOG2E = 1.4426950408889634
SCORE2 = SCALE * LOG2E
SAFE_BOUND = 50.0
F32 = jnp.float32
BF16 = jnp.bfloat16


def plan_items(mask):
    on = jnp.where(mask > 0, 1.0, 0.0)
    totals = jnp.sum(jnp.sum(on, axis=1), axis=1, keepdims=True)
    shape = (HEADS, HEAD_DIM)
    head = lax.broadcasted_iota(jnp.int32, shape, 0)
    lane = lax.broadcasted_iota(jnp.int32, shape, 1)
    across = jnp.sum(jnp.where(head == lane, totals, 0.0), axis=0, keepdims=True)
    ahead = (across > totals) | ((across == totals) & (lane < head))
    rank = jnp.sum(jnp.where(ahead & (lane < HEADS), 1.0, 0.0), axis=1, keepdims=True)
    wanted = jnp.where(lane < 2 * SPLITS, lane >> 1, lane - SPLITS).astype(F32)
    return jnp.sum(jnp.where(rank == wanted, head.astype(F32), 0.0), axis=0, keepdims=True).astype(jnp.int32)


def pack_kernel(
    mask_ref, q_ref, k_ref, v_ref, o_ref, out_ref, plan_ref,
    wide, tall, heads_ref, in_sems, out_sems, plan_sem,
):
    rows = q_ref.shape[0]
    part = rows // CHUNK
    loads, stores = [], []
    for which, src in enumerate((q_ref, k_ref, v_ref, o_ref)):
        for c in range(CHUNK):
            at = pl.ds(c * part, part)
            copy = pltpu.make_async_copy(src.at[at], wide.at[which, at], in_sems.at[which, c])
            copy.start()
            loads.append(copy)
    plan_ref[...] = jnp.broadcast_to(plan_items(mask_ref[...]), plan_ref.shape)
    copy = pltpu.make_async_copy(plan_ref, heads_ref, plan_sem)
    copy.start()
    copy.wait()
    for which in range(4):
        for c in range(CHUNK):
            loads[which * CHUNK + c].wait()

        def move(slot, carry, which=which):
            at = pl.multiple_of(heads_ref[0, slot] * HEAD_DIM, HEAD_DIM)
            tall[which, slot] = wide[which, :, pl.ds(at, HEAD_DIM)]
            return carry

        lax.fori_loop(0, ITEMS, move, 0, unroll=4)
        copy = pltpu.make_async_copy(tall.at[which], out_ref.at[:, which], out_sems.at[which])
        copy.start()
        stores.append(copy)
    for copy in stores:
        copy.wait()


def pack(block_masks, q_raw, k_raw, values, grad_out):
    rows, width = q_raw.shape
    vmem = pl.BlockSpec(memory_space=pltpu.VMEM)
    hbm = pl.BlockSpec(memory_space=pltpu.HBM)
    return pl.pallas_call(
        pack_kernel,
        out_shape=(
            jax.ShapeDtypeStruct((ITEMS, 4, rows, HEAD_DIM), BF16),
            jax.ShapeDtypeStruct((8, HEAD_DIM), jnp.int32),
        ),
        in_specs=[vmem] + [hbm] * 4,
        out_specs=(hbm, vmem),
        scratch_shapes=[
            pltpu.VMEM((4, rows, width), BF16),
            pltpu.VMEM((4, ITEMS, rows, HEAD_DIM), BF16),
            pltpu.SMEM((8, HEAD_DIM), jnp.int32),
            pltpu.SemaphoreType.DMA((4, CHUNK)),
            pltpu.SemaphoreType.DMA((4,)),
            pltpu.SemaphoreType.DMA,
        ],
        compiler_params=pltpu.CompilerParams(vmem_limit_bytes=60 * 2**20),
        name="pack_heads",
    )(block_masks, q_raw, k_raw, values, grad_out)


def inv_spread(raw_float):
    return lax.rsqrt(jnp.mean(raw_float * raw_float, axis=-1, keepdims=True) + NORM_EPS)


def norm_back(raw_float, gain, grad_normed):
    inv = inv_spread(raw_float)
    unit = raw_float * inv
    scaled = gain * grad_normed
    inner = jnp.sum(scaled * unit, axis=-1, keepdims=True) * (1.0 / HEAD_DIM)
    return (scaled - unit * inner) * inv, grad_normed * unit


def fold_rows(full):
    return jnp.sum(full.reshape(-1, 8, full.shape[-1]), axis=0)


def item_kernel(
    nb, info_ref, list_ref, mask_ref, gain_ref, hbm_ref, qk_ref, v_ref, part_ref,
    in_ref, qk_out, v_out, in_sems, qk_sems, v_sems, kv, kt, pairs_even, pairs_odd, acc, left, right, grad_qt, shifts,
):
    first, last, careful = info_ref[0], info_ref[1], info_ref[2]
    q_gain = gain_ref[0:1, :]
    k_gain = gain_ref[1:2, :]
    slots = list_ref.shape[0] // nb
    zero_half = jnp.zeros((BLOCK, HEAD_DIM), BF16)

    def load(step):
        at = pl.ds(step * UNROLL, UNROLL)
        return pltpu.make_async_copy(hbm_ref.at[at], in_ref.at[at], in_sems.at[step])

    def store(step):
        at = pl.ds(step * UNROLL, UNROLL)
        return (
            pltpu.make_async_copy(qk_out.at[at], qk_ref.at[at], qk_sems.at[step]),
            pltpu.make_async_copy(v_out.at[at], v_ref.at[at], v_sems.at[step]),
        )

    for step in range(nb // UNROLL):
        load(step).start()

    def prepare_keys(step, carry):
        load(step).wait()
        for u in range(UNROLL):
            j = step * UNROLL + u
            raw = in_ref[j, 1].astype(F32)
            normed = (raw * inv_spread(raw) * k_gain).astype(BF16)
            kv[j, :, :HEAD_DIM] = normed
            kv[j, :, HEAD_DIM:] = in_ref[j, 2]
            kt[j] = normed.T
            acc[j] = jnp.zeros((BLOCK, 2 * HEAD_DIM), F32)
            qk_out[j, 0] = zero_half
            shifts[j] = jnp.zeros((8, BLOCK), F32)
        return carry

    def prepare_query(i, padded):
        raw = in_ref[i, 0].astype(F32)
        normed = (raw * inv_spread(raw) * q_gain).astype(BF16)
        o_block = in_ref[i, 3]
        left[i, :HEAD_DIM, :BLOCK] = normed.T
        left[i, HEAD_DIM:, BLOCK:] = o_block.T
        right[i, :BLOCK, :HEAD_DIM] = o_block
        right[i, BLOCK:, HEAD_DIM:] = normed
        if padded:
            left[i, :HEAD_DIM, BLOCK:] = zero_half
            left[i, HEAD_DIM:, :BLOCK] = zero_half
            right[i, :BLOCK, HEAD_DIM:] = zero_half
            right[i, BLOCK:, :HEAD_DIM] = zero_half

    def prepare_queries(step, carry):
        for u in range(UNROLL):
            prepare_query(first + step * UNROLL + u, True)
        return carry

    def finish_key(j):
        grad, gains = norm_back(in_ref[j, 1].astype(F32), k_gain, acc[j, :, HEAD_DIM:] * SCALE)
        qk_out[j, 1] = grad.astype(BF16)
        v_out[j] = acc[j, :, :HEAD_DIM].astype(BF16)
        return fold_rows(gains)

    def finish_keys(step, total):
        for u in range(UNROLL):
            total = total + finish_key(step * UNROLL + u)
        for copy in store(step):
            copy.start()
        return total

    def finish_query(i, total_qt):
        grad, gains = norm_back(in_ref[i, 0].astype(F32), q_gain, total_qt.T * SCALE)
        qk_out[i, 0] = grad.astype(BF16)
        return fold_rows(gains)

    lax.fori_loop(0, nb // UNROLL, prepare_keys, 0)
    dense = info_ref[3]
    ahead = jnp.where((dense == 0) | (careful > 0), last - first, 0)
    lax.fori_loop(0, ahead // UNROLL, prepare_queries, 0)
    kv[nb] = jnp.zeros((BLOCK, 2 * HEAD_DIM), BF16)
    kt[nb] = zero_half
    acc[nb] = jnp.zeros((BLOCK, 2 * HEAD_DIM), F32)

    part_ref[...] = jnp.zeros((16, HEAD_DIM), F32)

    @pl.when(careful > 0)
    def _():
        def peak_row(i, carry):
            def peak_step(at, peak):
                j = list_ref[i * slots + at]
                scores = jnp.dot(kv[j, :, :HEAD_DIM], left[i, :HEAD_DIM, :BLOCK], preferred_element_type=F32)
                return jnp.maximum(peak, jnp.max(scores.reshape(-1, 8, BLOCK), axis=0))

            peak = lax.fori_loop(0, info_ref[8 + i], peak_step, jnp.full((8, BLOCK), NEG_FILL, F32))
            shifts[i] = jnp.broadcast_to(jnp.max(peak, axis=0, keepdims=True) * SCORE2, (8, BLOCK))
            return carry

        lax.fori_loop(first, last, peak_row, 0)

    def score_group(pairs, i, places, stats):
        total, dotted = stats
        shift = shifts[i, 0:1, :]
        for at, j, allowed in places:
            both = jnp.dot(kv[j], left[i], preferred_element_type=F32)
            weights = jnp.exp2(both[:, :BLOCK] * SCORE2 + (jnp.where(allowed, 0.0, NEG_FILL) - shift))
            grads = both[:, BLOCK:]
            pairs[at, :, :BLOCK] = weights
            pairs[at, :, BLOCK : 2 * BLOCK] = grads
            total = total + fold_rows(weights)
            dotted = dotted + fold_rows(weights * grads)
        return total, dotted

    def grad_group(pairs, i, places, inv_total, row_delta, total_qt):
        halves, keys = [], []
        for at, j, _ in places:
            weights = pairs[at, :, :BLOCK] * inv_total
            half = (weights * (pairs[at, :, BLOCK : 2 * BLOCK] - row_delta)).astype(BF16)
            acc[j] += jnp.dot(
                jnp.concatenate([weights.astype(BF16), half], axis=1), right[i], preferred_element_type=F32
            )
            halves.append(half)
            keys.append(kt[j])
        return total_qt + jnp.dot(
            jnp.concatenate(keys, axis=1), jnp.concatenate(halves, axis=0), preferred_element_type=F32
        )

    zero = jnp.zeros((8, BLOCK), F32)
    no_grad = jnp.zeros((HEAD_DIM, BLOCK), F32)

    def row_scales(stats):
        total, dotted = stats
        inv_total = 1.0 / jnp.sum(total, axis=0, keepdims=True)
        return inv_total, jnp.sum(dotted, axis=0, keepdims=True) * inv_total

    def in_turn(start, stop, stats, visit):
        def two_visits(step, stats):
            i = start + 2 * step
            stats = visit(i, i + 1, pairs_even, pairs_odd, stats)
            return visit(i + 1, jnp.minimum(i + 2, stop - 1), pairs_odd, pairs_even, stats)

        lax.fori_loop(0, (stop - start) // 2, two_visits, stats)

    def attend_all():
        wide = 2 * BLOCK
        earlier = lax.broadcasted_iota(jnp.int32, (1, wide), 1) < BLOCK
        top, low = slice(0, BLOCK), slice(BLOCK, wide)

        def score_two(pairs, two):
            i = 2 * two
            queries = jnp.concatenate([left[i, top, top], left[i + 1, top, top]], axis=1)
            outs = jnp.concatenate([left[i, low, low], left[i + 1, low, low]], axis=1)
            shift = jnp.concatenate([shifts[i, 0:1, :], shifts[i + 1, 0:1, :]], axis=1)
            total = dotted = jnp.zeros((8, wide), F32)
            for j in range(nb):
                scores = jnp.dot(kv[j, :, :HEAD_DIM], queries, preferred_element_type=F32)
                grads = jnp.dot(kv[j, :, HEAD_DIM:], outs, preferred_element_type=F32)
                bias = jnp.where(
                    earlier,
                    jnp.where(mask_ref[i * nb + j] > 0, 0.0, NEG_FILL),
                    jnp.where(mask_ref[(i + 1) * nb + j] > 0, 0.0, NEG_FILL),
                )
                weights = jnp.exp2(scores * SCORE2 + (bias - shift))
                pairs[j, :, :wide] = weights
                pairs[j, :, wide:] = grads
                total = total + fold_rows(weights)
                dotted = dotted + fold_rows(weights * grads)
            return total, dotted

        def grads_of_two(mine, two, stats):
            i = 2 * two
            inv_total, row_delta = row_scales(stats)
            outs = jnp.concatenate([right[i, top, top], right[i + 1, top, top]], axis=0)
            queries = jnp.concatenate([right[i, low, low], right[i + 1, low, low]], axis=0)
            halves = []
            for j in range(nb):
                weights = mine[j, :, :wide] * inv_total
                half = (weights * (mine[j, :, wide:] - row_delta)).astype(BF16)
                acc[j, :, :HEAD_DIM] += jnp.dot(weights.astype(BF16), outs, preferred_element_type=F32)
                acc[j, :, HEAD_DIM:] += jnp.dot(half, queries, preferred_element_type=F32)
                halves.append(half)
            return jnp.dot(
                jnp.concatenate([kt[j] for j in range(nb)], axis=1),
                jnp.concatenate(halves, axis=0),
                preferred_element_type=F32,
            )

        def finish_two(two, total_qt):
            part_ref[0:8, :] += finish_query(2 * two, total_qt[:, :BLOCK]) + finish_query(
                2 * two + 1, total_qt[:, BLOCK:]
            )

        def visit(two, mine, other, stats):
            for u in range(2):
                prepare_query(2 * two + 2 + u, False)
            total_qt = grads_of_two(mine, two, stats)
            stats = score_two(other, two + 1)
            finish_two(two, total_qt)
            return stats

        for u in range(2):
            prepare_query(first + u, False)
        start, stop = first // 2, last // 2

        def two_visits(step, stats):
            stats = visit(start + 2 * step, pairs_even, pairs_odd, stats)
            return visit(start + 2 * step + 1, pairs_odd, pairs_even, stats)

        stats = lax.fori_loop(0, (stop - start) // 2 - 1, two_visits, score_two(pairs_even, start))
        stats = visit(stop - 2, pairs_even, pairs_odd, stats)
        finish_two(stop - 1, grads_of_two(pairs_odd, stop - 1, stats))
        total = zero
        for step in range(nb // UNROLL):
            total = finish_keys(step, total)
        part_ref[8:16, :] += total

    def attend_listed():
        def clear(at, carry):
            pairs_even[at, :, : 2 * BLOCK] = jnp.zeros((BLOCK, 2 * BLOCK), F32)
            pairs_odd[at, :, : 2 * BLOCK] = jnp.zeros((BLOCK, 2 * BLOCK), F32)
            return carry

        lax.fori_loop(0, 2 * GROUP + DENSE_FROM, clear, 0)

        def groups_of(i):
            return (info_ref[8 + i] + (GROUP - 1)) // GROUP

        def places(i, g):
            spots = [g * GROUP + u for u in range(GROUP)]
            return [(at, list_ref[i * slots + at], at < info_ref[8 + i]) for at in spots]

        def query_block(i, later, mine, other, stats):
            inv_total, row_delta = row_scales(stats)

            def step(g, carry):
                total_qt, total, dotted = carry
                total_qt = grad_group(mine, i, places(i, g), inv_total, row_delta, total_qt)
                return (total_qt, *score_group(other, later, places(later, g), (total, dotted)))

            total_qt, total, dotted = lax.fori_loop(
                0, jnp.maximum(groups_of(i), groups_of(later)), step, (no_grad, zero, zero)
            )
            grad_qt[i] = total_qt
            return total, dotted

        stats = lax.fori_loop(
            0, groups_of(first), lambda g, s: score_group(pairs_even, first, places(first, g), s), (zero, zero)
        )
        in_turn(first, last, stats, query_block)

    pl.when(dense > 0)(attend_all)
    pl.when(dense == 0)(attend_listed)

    def finish_queries(step, total):
        for u in range(UNROLL):
            i = first + step * UNROLL + u
            total = total + finish_query(i, grad_qt[i])
        return total

    behind = jnp.where(dense == 0, last - first, 0)
    part_ref[0:8, :] += lax.fori_loop(0, behind // UNROLL, finish_queries, zero)
    part_ref[8:16, :] += lax.fori_loop(0, jnp.where(dense == 0, nb // UNROLL, 0), finish_keys, zero)
    for step in range(nb // UNROLL):
        for copy in store(step):
            copy.wait()


def item_grads(info, block_list, mask, gains, arrived):
    nb = arrived.shape[0]
    slots = block_list.shape[0] // nb
    smem = pl.BlockSpec(memory_space=pltpu.SMEM)
    vmem = pl.BlockSpec(memory_space=pltpu.VMEM)
    hbm = pl.BlockSpec(memory_space=pltpu.HBM)
    return pl.pallas_call(
        functools.partial(item_kernel, nb),
        out_shape=(
            jax.ShapeDtypeStruct((nb, 2, BLOCK, HEAD_DIM), BF16),
            jax.ShapeDtypeStruct((nb, BLOCK, HEAD_DIM), BF16),
            jax.ShapeDtypeStruct((16, HEAD_DIM), F32),
        ),
        in_specs=[smem, smem, smem, vmem, hbm],
        out_specs=(hbm, hbm, vmem),
        scratch_shapes=[
            pltpu.VMEM((nb, 4, BLOCK, HEAD_DIM), BF16),
            pltpu.VMEM((nb, 2, BLOCK, HEAD_DIM), BF16),
            pltpu.VMEM((nb, BLOCK, HEAD_DIM), BF16),
            pltpu.SemaphoreType.DMA((nb // UNROLL,)),
            pltpu.SemaphoreType.DMA((nb // UNROLL,)),
            pltpu.SemaphoreType.DMA((nb // UNROLL,)),
            pltpu.VMEM((nb + 1, BLOCK, 2 * HEAD_DIM), BF16),
            pltpu.VMEM((nb + 1, HEAD_DIM, BLOCK), BF16),
            pltpu.VMEM((slots, BLOCK, 4 * BLOCK), F32),
            pltpu.VMEM((slots, BLOCK, 4 * BLOCK), F32),
            pltpu.VMEM((nb + 1, BLOCK, 2 * HEAD_DIM), F32),
            pltpu.VMEM((nb, 2 * HEAD_DIM, 2 * BLOCK), BF16),
            pltpu.VMEM((nb, 2 * BLOCK, 2 * HEAD_DIM), BF16),
            pltpu.VMEM((nb, HEAD_DIM, BLOCK), F32),
            pltpu.VMEM((nb, 8, BLOCK), F32),
        ],
        compiler_params=pltpu.CompilerParams(vmem_limit_bytes=60 * 2**20),
        name="item_grads",
    )(info, block_list, mask, gains, arrived)


def merge_kernel(count, tail_scale, heads_ref, in_ref, *out_refs):
    outs = out_refs[:count]

    def piece(slot, which):
        return in_ref[slot, which * BLOCK : (which + 1) * BLOCK, :]

    def pair(p, carry):
        at = pl.multiple_of(heads_ref[2 * p] * HEAD_DIM, HEAD_DIM)
        for which, out in enumerate(outs):
            both = piece(2 * p, which).astype(F32) + piece(2 * p + 1, which).astype(F32)
            out[:, pl.ds(at, HEAD_DIM)] = both.astype(BF16)
        return carry

    def single(slot, carry):
        at = pl.multiple_of(heads_ref[slot] * HEAD_DIM, HEAD_DIM)
        for which, out in enumerate(outs):
            out[:, pl.ds(at, HEAD_DIM)] = piece(slot, which)
        return carry

    lax.fori_loop(0, SPLITS, pair, 0, unroll=4)
    lax.fori_loop(2 * SPLITS, ITEMS, single, 0, unroll=4)
    if len(out_refs) > count:
        def tail(slot, total):
            return total + in_ref[slot, count * BLOCK : count * BLOCK + 16, :].astype(F32)

        total = lax.fori_loop(0, ITEMS, tail, jnp.zeros((16, HEAD_DIM), F32), unroll=8)
        out_refs[count][...] = (total[0:2] + (total[2:4] + total[4:6])) * tail_scale


def merge(item_heads, returned, count, tail_scale=None):
    vmem = pl.BlockSpec(memory_space=pltpu.VMEM)
    wide = jax.ShapeDtypeStruct((BLOCK, HEADS * HEAD_DIM), BF16)
    shapes = (wide,) * count + ((jax.ShapeDtypeStruct((2, HEAD_DIM), F32),) if tail_scale else ())
    return pl.pallas_call(
        functools.partial(merge_kernel, count, tail_scale),
        out_shape=shapes,
        in_specs=[pl.BlockSpec(memory_space=pltpu.SMEM), vmem],
        out_specs=(vmem,) * len(shapes),
        compiler_params=pltpu.CompilerParams(vmem_limit_bytes=24 * 2**20),
        name="merge_heads",
    )(item_heads, returned)


def attach_kernel(part_ref, v_ref, out_ref):
    total = part_ref[...]
    high = total.astype(BF16)
    rest = total - high.astype(F32)
    middle = rest.astype(BF16)
    low = (rest - middle.astype(F32)).astype(BF16)
    pieces = [high.astype(F32), middle.astype(F32), low.astype(F32), jnp.zeros((10, HEAD_DIM), F32)]
    tail = jnp.concatenate(pieces, axis=0).astype(BF16)

    def move(slot, carry):
        out_ref[slot, :BLOCK, :] = v_ref[slot]
        out_ref[slot, BLOCK:, :] = tail
        return carry

    lax.fori_loop(0, ITEMS, move, 0)


def attach(part, grads_v):
    vmem = pl.BlockSpec(memory_space=pltpu.VMEM)
    return pl.pallas_call(
        attach_kernel,
        out_shape=jax.ShapeDtypeStruct((ITEMS, BLOCK + 16, HEAD_DIM), BF16),
        in_specs=[vmem, vmem],
        out_specs=vmem,
        name="attach_gains",
    )(part, grads_v)


def sum_over_videos(part):
    count = lax.axis_size("dp")
    step = 1
    while step < count:
        part = part + lax.ppermute(part, "dp", [(i, i ^ step) for i in range(count)])
        step *= 2
    return part


def block_lists(mask_head):
    nb = mask_head.shape[0]
    on = (mask_head > 0).astype(jnp.int32)
    lower = (jnp.arange(nb)[:, None] < jnp.arange(nb)[None, :]).astype(jnp.int32)
    place = jnp.sum(on[:, :, None] * lower[None, :, :], axis=1)
    slot = jnp.arange(nb, dtype=jnp.int32)
    hit = (on[:, :, None] > 0) & (place[:, :, None] == slot[None, None, :])
    which = jnp.arange(nb, dtype=jnp.int32)[None, :, None]
    counts = jnp.sum(on, axis=1)
    lists = nb + jnp.sum(jnp.where(hit, which - nb, 0), axis=1)
    return counts, lists


def body(q_raw, k_raw, values, grad_out, q_gain, k_gain, block_masks):
    device_rank = lax.axis_index("ulysses")
    tok_rows, width = q_raw.shape[1:]
    nb = block_masks.shape[1]
    seq_len = tok_rows * lax.axis_size("ulysses")
    videos = lax.axis_size("dp")
    outgoing, plan = pack(block_masks, q_raw[0], k_raw[0], values[0], grad_out[0])
    item_heads = plan[0, :ITEMS]
    arrived = lax.all_to_all(outgoing, "ulysses", split_axis=0, concat_axis=0, tiled=True)
    head = lax.dynamic_index_in_dim(item_heads, device_rank, 0, keepdims=False)
    mask_head = lax.dynamic_index_in_dim(block_masks, head, 0, keepdims=False)
    counts, lists = block_lists(mask_head)
    split = device_rank < 2 * SPLITS
    half = device_rank % 2
    first = jnp.where(split, half * (nb // 2), 0)
    last = jnp.where(split, (half + 1) * (nb // 2), nb)
    bound = 1.02 * HEAD_DIM * SCORE2 * jnp.max(jnp.abs(q_gain)) * jnp.max(jnp.abs(k_gain))
    careful = jnp.where(bound < SAFE_BOUND, 0, 1)
    dense = jnp.where(jnp.max(counts) > DENSE_FROM, 1, 0)
    info = jnp.concatenate(
        [jnp.stack([first, last, careful, dense]).astype(jnp.int32), jnp.zeros((4,), jnp.int32), counts]
    )
    gains = jnp.stack([q_gain, k_gain])
    grads_qk, grads_v, part = item_grads(info, lists.reshape(-1), mask_head.reshape(-1), gains, arrived)
    back_qk = lax.all_to_all(
        grads_qk.reshape(nb, 2 * BLOCK, HEAD_DIM), "ulysses", split_axis=0, concat_axis=0, tiled=True
    )
    part = sum_over_videos(jnp.sum(part.reshape(2, 8, HEAD_DIM), axis=1))
    attached, back_qk = lax.optimization_barrier((attach(part, grads_v), back_qk))
    back_v = lax.all_to_all(attached, "ulysses", split_axis=0, concat_axis=0, tiled=True)
    grad_q, grad_k = merge(item_heads, back_qk, 2)
    grad_v, gain_grads = merge(item_heads, back_v, 1, (videos * seq_len * HEADS) ** (-0.5))
    return (grad_q[None], grad_k[None], grad_v[None], gain_grads)


def solution(mesh):
    tokens = P("dp", "ulysses", None)
    return jax.shard_map(
        body,
        mesh=mesh,
        in_specs=(tokens, tokens, tokens, tokens, P(), P(), P()),
        out_specs=(tokens, tokens, tokens, P()),
        check_vma=False,
    )
```
